32 devices in a mesh: dp: 4 (over y, core), fsdp: 8 (over z, x).
Axes of the slice: x: 2, y: 2, z: 4, core: 2. Of those that a mesh axis runs over, the one named last changes fastest.
Arguments:
- tokens: bfloat16 [2, 16384, 768], P(None, ('dp', 'fsdp')), may hold values from -6 to 6
- cotangent: bfloat16 [2, 16384, 768], P(None, ('dp', 'fsdp')), may hold values from -6 to 6
- seg_lengths: int32 [2, 32, 8], P(None, ('dp', 'fsdp')), may hold values from 0 to 512, as said below
- bucket_of: int32 [1023], replicated, may hold values from 0 to 31, as said below
- attn_w: float32 [4, 768, 768], P(None, 'fsdp'), may hold values from -1.4433757 to 1.4433757
- attn_m: float32 [4, 768, 768], P(None, 'fsdp'), may hold values from -362.03867 to 362.03867
- attn_v: float32 [4, 768, 768], P(None, 'fsdp'), may hold values from 1.31072 to 655.36
- ffin_w: float32 [768, 3072], P('fsdp'), may hold values from -0.28867513 to 0.28867513
- ffin_m: float32 [768, 3072], P('fsdp'), may hold values from -54.3058 to 54.3058
- ffin_v: float32 [768, 3072], P('fsdp'), may hold values from 1.31072 to 13.1072
- ffout_w: float32 [3072, 768], P('fsdp'), may hold values from -0.14433757 to 0.14433757
- ffout_m: float32 [3072, 768], P('fsdp'), may hold values from -90.50967 to 90.50967
- ffout_v: float32 [3072, 768], P('fsdp'), may hold values from 3.2768 to 52.4288
- gains: float32 [2, 768], P(None, 'fsdp'), may hold values from 0.2 to 2.6
- gains_m: float32 [2, 768], P(None, 'fsdp'), may hold values from -162.9174 to 162.9174
- gains_v: float32 [2, 768], P(None, 'fsdp'), may hold values from 29.4912 to 134.3488
- table: float32 [32, 12], P('fsdp'), may hold values from -8 to 8
- table_m: float32 [32, 12], P('fsdp'), may hold values from -633.5677 to 633.5677
- table_v: float32 [32, 12], P('fsdp'), may hold values from 491.52 to 2129.92
Outputs:
- block_out: bfloat16 [2, 16384, 768], P(None, ('dp', 'fsdp'))
- grad_in: bfloat16 [2, 16384, 768], P(None, ('dp', 'fsdp'))
- attn_new: float32 [4, 768, 768], P(None, 'fsdp')
- attn_m_new: float32 [4, 768, 768], P(None, 'fsdp')
- attn_v_new: float32 [3, 768, 768], P(None, 'fsdp')
- out_v_new: float32 [768, 768], P('fsdp')
- ffin_new: float32 [768, 3072], P('fsdp')
- ffin_m_new: float32 [768, 3072], P('fsdp')
- ffin_v_new: float32 [768, 3072], P('fsdp')
- ffout_new: float32 [3072, 768], P('fsdp')
- ffout_m_new: float32 [3072, 768], P('fsdp')
- ffout_v_new: float32 [3072, 768], P('fsdp')
- gains_new: float32 [2, 768], P(None, 'fsdp')
- gains_m_new: float32 [2, 768], P(None, 'fsdp')
- gains_v_new: float32 [2, 768], P(None, 'fsdp')
- table_new: float32 [32, 12], P('fsdp')
- table_m_new: float32 [32, 12], P('fsdp')
- table_v_new: float32 [32, 12], P('fsdp')
- norms: float32 [9, 2], replicated
The draws below stay inside these ranges and needn't reach their ends.
Inputs may be any that keep to these rules, and one draw needn't show every extreme that they name: `seg_lengths`: each row of 8 lengths describes one block: either one passage (the first length from 128 to 512, the others 0) or 8 queries of 512 // 64 (at least 1) to 64 rows each. A row's lengths sum to at most 512; rows past the sum are padding. In every micro-batch some passage fills its block. bucket_of[o + 511] is the bucket of a key o rows after its query: |o| itself for |o| < 8, else 8 plus the number of seven increasing bounds, between 9 and 256, that |o| reaches; 16 is added where o > 0. It never falls as |o| grows on either side.
All inputs are finite; a program needn't handle non-finite values.
Results may differ from the reference program's by a relative error of at most 0.014.
The reference program's roundings to bfloat16 on the way count: a program that leaves them out, or rounds other values in their place, can miss the bound.
Values may be sent and summed in bfloat16 or wider, within the bound.
No kernel may reach another device: no remote copies, remote signals or barrier semaphores. Data moves between devices by JAX's collectives and lax.ppermute only.
A program may use at most 256 MiB of HBM per device.

```python
import math
import jax
import jax.numpy as jnp
from jax import lax

D = 768
HEADS = 12
HD = 64
FF = 3072
BUCKETS = 32
ROWS = 512
SEGS = 8
MB = 2
STEP = 5
TOKENS = 16384


def ramp(count, ratio):
    places = jnp.arange(count, dtype=jnp.float32) / max(count - 1, 1)
    level = jnp.exp(places * math.log(ratio))
    return level / math.sqrt((ratio * ratio - 1.0) / (2.0 * math.log(ratio)))


def normal_noise(key, shape):
    return jax.random.truncated_normal(key, -4.0, 4.0, shape, jnp.float32)


def positive_spread(key, shape):
    return jnp.exp(jax.random.uniform(key, shape, jnp.float32, -0.6931472, 0.6931472))


def grad_size():
    return math.sqrt(MB * TOKENS)


def draw_seg_lengths(key, part):
    key = jax.random.fold_in(key, 3)
    keys = jax.random.split(key, 4)
    blocks = TOKENS // ROWS
    kinds = jax.random.randint(keys[0], (MB, blocks), 0, 2)
    passage = jax.random.randint(keys[1], (MB, blocks), ROWS // 4, ROWS + 1)
    chosen = jax.random.randint(keys[2], (MB,), 0, blocks)
    forced = jnp.arange(blocks, dtype=jnp.int32)[None, :] == chosen[:, None]
    kinds = jnp.where(forced, 1, kinds)
    passage = jnp.where(forced, ROWS, passage)
    queries = jax.random.randint(keys[3], (MB, blocks, SEGS), max(1, ROWS // 64), ROWS // 8 + 1)
    first_slot = (jnp.arange(SEGS, dtype=jnp.int32) == 0)[None, None, :]
    passage_row = jnp.where(first_slot, passage[:, :, None], 0)
    return jnp.where(kinds[:, :, None] == 1, passage_row, queries).astype(jnp.int32)


def draw_bucket_of(key, part):
    key = jax.random.fold_in(key, 5)
    exact = BUCKETS // 4
    order = jax.random.permutation(key, ROWS // 2 - exact)[:exact - 1]
    marks = jnp.sort(order).astype(jnp.int32) + exact + 1
    offsets = jnp.arange(2 * ROWS - 1, dtype=jnp.int32) - (ROWS - 1)
    distance = jnp.abs(offsets)
    far_bucket = exact + jnp.sum((distance[:, None] >= marks[None, :]).astype(jnp.int32), axis=1)
    near = jnp.where(distance < exact, distance, far_bucket)
    return (near + BUCKETS // 2 * (offsets > 0).astype(jnp.int32)).astype(jnp.int32)


def draw_attn_w(key, part):
    key = jax.random.fold_in(key, 11)
    base = normal_noise(key, (4, D, D))
    ratio = 3.0
    scales = jnp.array([0.4, 0.4, 1.0, 5.0], jnp.float32)[:, None, None] / math.sqrt(D)
    return base * scales * ramp(D, ratio)[None, :, None]


def draw_attn_m(key, part):
    key = jax.random.fold_in(key, 12)
    base = normal_noise(key, (4, D, D))
    ratio = 3.0
    scales = jnp.array([2.0, 2.0, 1.0, 0.3], jnp.float32)[:, None, None] * 0.111 * grad_size()
    return base * scales * ramp(D, ratio)[None, :, None]


def draw_attn_v(key, part):
    key = jax.random.fold_in(key, 13)
    sizes = jnp.array([2.0, 2.0, 1.0, 0.3], jnp.float32)[:, None, None] * grad_size()
    return positive_spread(key, (4, D, D)) * 0.002 * sizes * sizes


def draw_ffin_w(key, part):
    key = jax.random.fold_in(key, 21)
    base = normal_noise(key, (D, FF))
    ratio = 3.0
    return base * ramp(D, ratio)[:, None] / math.sqrt(D)


def draw_ffin_m(key, part):
    key = jax.random.fold_in(key, 22)
    base = normal_noise(key, (D, FF))
    ratio = 3.0
    return base * ramp(D, ratio)[:, None] * 0.111 * 0.3 * grad_size()


def draw_ffin_v(key, part):
    key = jax.random.fold_in(key, 23)
    size = 0.3 * grad_size()
    return positive_spread(key, (D, FF)) * 0.002 * size * size


def draw_ffout_w(key, part):
    key = jax.random.fold_in(key, 31)
    base = normal_noise(key, (FF, D))
    ratio = 3.0
    return base * ramp(FF, ratio)[:, None] / math.sqrt(FF)


def draw_ffout_m(key, part):
    key = jax.random.fold_in(key, 32)
    base = normal_noise(key, (FF, D))
    ratio = 3.0
    return base * ramp(FF, ratio)[:, None] * 0.111 * 0.6 * grad_size()


def draw_ffout_v(key, part):
    key = jax.random.fold_in(key, 33)
    size = 0.6 * grad_size()
    return positive_spread(key, (FF, D)) * 0.002 * size * size


def draw_gains(key, part):
    key = jax.random.fold_in(key, 41)
    base = normal_noise(key, (2, D))
    ratio = 3.0
    return (1.0 + 0.1 * base) * ramp(D, ratio)[None, :]


def draw_gains_m(key, part):
    key = jax.random.fold_in(key, 42)
    base = normal_noise(key, (2, D))
    ratio = 3.0
    return base * ramp(D, ratio)[None, :] * 0.111 * grad_size()


def draw_gains_v(key, part):
    key = jax.random.fold_in(key, 43)
    size = grad_size()
    return positive_spread(key, (2, D)) * 0.002 * size * size


def draw_table(key, part):
    key = jax.random.fold_in(key, 51)
    base = normal_noise(key, (BUCKETS, HEADS))
    ratio = 3.0
    return base * ramp(BUCKETS, ratio)[:, None]


def draw_table_m(key, part):
    key = jax.random.fold_in(key, 52)
    base = normal_noise(key, (BUCKETS, HEADS))
    ratio = 3.0
    return base * ramp(BUCKETS, ratio)[:, None] * 0.111 * 4.0 * grad_size()


def draw_table_v(key, part):
    key = jax.random.fold_in(key, 53)
    size = 4.0 * grad_size()
    return positive_spread(key, (BUCKETS, HEADS)) * 0.002 * size * size


def steps_of(key, extent, shards, low, high):
    def one(axis_at, parts):
        steps = jax.random.uniform(jax.random.fold_in(jax.random.fold_in(key, 6), axis_at), (parts,), jnp.float32, low / len(shards), high / len(shards))
        return jnp.repeat(jnp.exp(steps), extent[axis_at] // parts).reshape((-1,) + (1,) * (len(extent) - axis_at - 1))

    loudness = one(*shards[0])
    for cut in shards[1:]:
        loudness = loudness * one(*cut)
    return loudness


def normal_values(key, extent, scale, limit, cuts=(), kind=jnp.bfloat16):
    loudness = steps_of(key, extent, cuts, -0.22, 0.18) if cuts else 1.0
    values = jax.random.normal(key, extent, jnp.float32) * scale * loudness
    return jnp.minimum(jnp.maximum(values, -limit), limit).astype(kind)


def setup_inputs(seed: int = 0) -> dict:
    arg_keys = jax.random.split(jax.random.key(seed), 20)
    return {
        "tokens": normal_values(arg_keys[0], (MB, TOKENS, D), 1.0, 6.0, ((1, 32),)),
        "cotangent": normal_values(arg_keys[1], (MB, TOKENS, D), 1.0, 6.0, ((1, 32),)),
        "seg_lengths": draw_seg_lengths(jax.random.fold_in(arg_keys[19], 71), 0),
        "bucket_of": draw_bucket_of(jax.random.fold_in(arg_keys[19], 71), 0),
        "attn_w": draw_attn_w(jax.random.fold_in(arg_keys[19], 71), 0),
        "attn_m": draw_attn_m(jax.random.fold_in(arg_keys[19], 71), 0),
        "attn_v": draw_attn_v(jax.random.fold_in(arg_keys[19], 71), 0),
        "ffin_w": draw_ffin_w(jax.random.fold_in(arg_keys[19], 71), 0),
        "ffin_m": draw_ffin_m(jax.random.fold_in(arg_keys[19], 71), 0),
        "ffin_v": draw_ffin_v(jax.random.fold_in(arg_keys[19], 71), 0),
        "ffout_w": draw_ffout_w(jax.random.fold_in(arg_keys[19], 71), 0),
        "ffout_m": draw_ffout_m(jax.random.fold_in(arg_keys[19], 71), 0),
        "ffout_v": draw_ffout_v(jax.random.fold_in(arg_keys[19], 71), 0),
        "gains": draw_gains(jax.random.fold_in(arg_keys[19], 71), 0),
        "gains_m": draw_gains_m(jax.random.fold_in(arg_keys[19], 71), 0),
        "gains_v": draw_gains_v(jax.random.fold_in(arg_keys[19], 71), 0),
        "table": draw_table(jax.random.fold_in(arg_keys[19], 71), 0),
        "table_m": draw_table_m(jax.random.fold_in(arg_keys[19], 71), 0),
        "table_v": draw_table_v(jax.random.fold_in(arg_keys[19], 71), 0),
    }


NORM_EPS = 1e-06
BETA_ONE = 0.9
BETA_TWO = 0.999
ADAM_EPS = 1e-06
DECAY = 0.01
RATE = 0.5
MASKED = -1000000000.0
HIGH = lax.Precision.HIGHEST
step_blocks = 8

@jax.custom_vjp
def low(v):
    return lax.optimization_barrier(v.astype(jnp.bfloat16)).astype(jnp.float32)

@jax.custom_vjp
def low_back(v):
    return v

def low_keep(v):
    return (low(v), None)

def low_pass(kept, grad):
    return (grad,)

def back_keep(v):
    return (v, None)

def back_low(kept, grad):
    return (low(grad),)
low.defvjp(low_keep, low_pass)
low_back.defvjp(back_keep, back_low)

def rms_norm(values, gain):
    return values * lax.rsqrt(lax.optimization_barrier(jnp.mean(values * values, axis=-1, keepdims=True)) + NORM_EPS) * gain

def row_labels(lengths, count):
    ends = jnp.cumsum(lengths).astype(jnp.int32)
    places = jnp.arange(count, dtype=jnp.int32)
    labels = lax.optimization_barrier(jnp.sum((places[:, None] >= ends[None, :]).astype(jnp.int32), axis=1))
    return (labels, places < ends[-1])

def block(rows_in, lengths, weights, bias_full):
    attn_full, ffin_full, ffout_full, gains_full = weights
    labels, valid = row_labels(lengths, ROWS)
    allowed = labels[:, None] == labels[None, :]
    normed = low(rms_norm(rows_in, gains_full[0]))
    split = [low_back(low(jnp.dot(normed, attn_full[which], precision=HIGH))).reshape(ROWS, HEADS, HD) for which in range(3)]
    scores = low_back(jnp.einsum('ihe,jhe->hij', split[0], split[1], precision=HIGH) + bias_full)
    scores = jnp.where(allowed[None], scores, MASKED)
    probs = low(jax.nn.softmax(scores, axis=-1))
    mixed = jnp.einsum('hij,jhe->ihe', probs, split[2], precision=HIGH).reshape(ROWS, D)
    mixed = low_back(low(mixed))
    middle = rows_in + low_back(jnp.dot(mixed, attn_full[3], precision=HIGH))
    normed_two = low(rms_norm(middle, gains_full[1]))
    inner = low_back(jnp.dot(normed_two, ffin_full, precision=HIGH))
    active = low(jax.nn.gelu(inner))
    return middle + low_back(jnp.dot(active, ffout_full, precision=HIGH))

def moments(weight, first, second, grad):
    first_new = BETA_ONE * first + (1.0 - BETA_ONE) * grad
    second_new = BETA_TWO * second + (1.0 - BETA_TWO) * grad * grad
    direction = first_new / (1.0 - BETA_ONE ** STEP) / (jnp.sqrt(second_new / (1.0 - BETA_TWO ** STEP)) + ADAM_EPS) + DECAY * weight
    return (first_new, second_new, direction)

def squares_of(arrays):
    attn_part, ffin_part, ffout_part, gain_part, table_part = arrays
    return jnp.concatenate([lax.optimization_barrier(jnp.sum(attn_part * attn_part, axis=(1, 2))), jnp.sum(ffin_part * ffin_part)[None], jnp.sum(ffout_part * ffout_part)[None], lax.optimization_barrier(jnp.sum(gain_part * gain_part, axis=1)), jnp.sum(table_part * table_part)[None]])

def reference(tokens, cotangent, seg_lengths, bucket_of, attn_w, attn_m, attn_v, ffin_w, ffin_m, ffin_v, ffout_w, ffout_m, ffout_v, gains, gains_m, gains_v, table, table_m, table_v):
    blocks = MB * (TOKENS // ROWS)
    groups = blocks // step_blocks
    inputs = tokens.astype(jnp.float32).reshape(groups, step_blocks, ROWS, D)
    lengths = seg_lengths.reshape(groups, step_blocks, SEGS)
    places = jnp.arange(ROWS, dtype=jnp.int32)
    offsets = places[None, :] - places[:, None] + ROWS - 1
    onehot = (bucket_of[None, :] == jnp.arange(BUCKETS, dtype=jnp.int32)[:, None]).astype(jnp.float32)

    def forward(inputs, attn_w, ffin_w, ffout_w, gains, table):
        weights = (low(attn_w), low(ffin_w), low(ffout_w), low(gains))
        bias_off = jnp.dot(low(table).T, onehot, precision=HIGH)
        bias_full = bias_off[:, offsets]

        def one_block(rows_in, lens):
            return block(rows_in, lens, weights, bias_full)

        def group(pair):
            return jax.vmap(one_block)(pair[0], pair[1])
        return lax.map(jax.checkpoint(group), (inputs, lengths))

    def valid_rows(lens):
        return row_labels(lens, ROWS)[1]
    valid = jax.vmap(jax.vmap(valid_rows))(lengths)
    upstream = cotangent.astype(jnp.float32).reshape(groups, step_blocks, ROWS, D) * valid[..., None].astype(jnp.float32)
    result, pullback = jax.vjp(forward, inputs, attn_w, ffin_w, ffout_w, gains, table)
    grad_x, grad_attn, grad_ffin, grad_ffout, grad_gains, grad_table = pullback(upstream)
    params = (attn_w, ffin_w, ffout_w, gains, table)
    firsts = (attn_m, ffin_m, ffout_m, gains_m, table_m)
    seconds = (attn_v, ffin_v, ffout_v, gains_v, table_v)
    grads = (grad_attn, grad_ffin, grad_ffout, grad_gains, grad_table)
    states = [moments(weight, first, second, grad) for weight, first, second, grad in zip(params, firsts, seconds, grads)]
    directions = tuple((item[2] for item in states))
    weight_norms = jnp.sqrt(squares_of(params))
    step_norms = jnp.sqrt(squares_of(directions))
    trust = weight_norms / (step_norms + ADAM_EPS)
    factors = (trust[0:4][:, None, None], trust[4], trust[5], trust[6:8][:, None], trust[8])
    fresh = [weight - RATE * factor * direction for weight, factor, direction in zip(params, factors, directions)]
    norms = jnp.stack([weight_norms, step_norms], axis=1)
    block_out = result.reshape(MB, TOKENS, D).astype(jnp.bfloat16)
    grad_in = grad_x.reshape(MB, TOKENS, D).astype(jnp.bfloat16)
    return (block_out, grad_in, fresh[0], states[0][0], states[0][1][:3], states[0][1][3], fresh[1], states[1][0], states[1][1], fresh[2], states[2][0], states[2][1], fresh[3], states[3][0], states[3][1], fresh[4], states[4][0], states[4][1], norms)
```

```python
import functools

import jax
import jax.numpy as jnp
from jax import lax
from jax.experimental import pallas as pl
from jax.experimental.pallas import tpu as pltpu
from jax.sharding import PartitionSpec as P

HEADS = 12
HD = 64
BUCKETS = 32
ROWS = 512
STEP = 5
WIDTH = 768
FF = 3072
PAIRS = HEADS // 2
LANES = 128
OFFS = 2 * ROWS
BAND = 3 * LANES

NORM_EPS = 1e-06
BETA_ONE = 0.9
BETA_TWO = 0.999
ADAM_EPS = 1e-06
DECAY = 0.01
RATE = 0.5
MASKED = -1000000000.0
MIB = 1024 * 1024

F32 = jnp.float32
BF16 = jnp.bfloat16


SLIGHT = pl.CostEstimate(flops=1, bytes_accessed=1, transcendentals=0)


def mm(a, b):
    return jnp.dot(a, b, preferred_element_type=F32)


def mm_nt(a, b):
    return lax.dot_general(a, b, (((1,), (1,)), ((), ())), preferred_element_type=F32)


def mm_tn(a, b):
    return lax.dot_general(a, b, (((0,), (0,)), ((), ())), preferred_element_type=F32)


def square(ref):
    return ref[...].reshape(WIDTH, WIDTH)


def inverse_rms(values):
    return lax.rsqrt(jnp.mean(values * values, axis=-1, keepdims=True) + NORM_EPS)


def norm_back(values, gain, grad):
    inv = inverse_rms(values)
    scaled = values * inv
    weighted = grad * gain
    inner = jnp.mean(weighted * scaled, axis=-1, keepdims=True)
    return inv * (weighted - scaled * inner), jnp.sum(grad * scaled, axis=0, keepdims=True)


def half_lanes(value, which):
    lane = lax.broadcasted_iota(jnp.int32, value.shape, 1)
    keep = lane < HD if which == 0 else lane >= HD
    return jnp.where(keep, value, jnp.zeros_like(value))


def project_kernel(x_ref, gain_ref, w_ref, out_ref, a1_ref):
    @pl.when(pl.program_id(0) == 0)
    def _():
        x = x_ref[...].astype(F32)
        a1_ref[...] = (x * inverse_rms(x) * gain_ref[...]).astype(BF16)

    out_ref[0] = mm(a1_ref[...], square(w_ref)).astype(BF16)


def project(x, gain, weights):
    rows = x.shape[0]
    parts, _, per, _ = weights.shape
    return pl.pallas_call(
        project_kernel,
        grid=(3,),
        in_specs=[
            pl.BlockSpec((rows, WIDTH), lambda k: (0, 0)),
            pl.BlockSpec((1, WIDTH), lambda k: (0, 0)),
            pl.BlockSpec((parts, 1, per, WIDTH), lambda k: (0, k, 0, 0)),
        ],
        out_specs=[
            pl.BlockSpec((1, rows, WIDTH), lambda k: (k, 0, 0)),
            pl.BlockSpec((rows, WIDTH), lambda k: (0, 0)),
        ],
        out_shape=[
            jax.ShapeDtypeStruct((3, rows, WIDTH), BF16),
            jax.ShapeDtypeStruct((rows, WIDTH), BF16),
        ],
        compiler_params=pltpu.CompilerParams(vmem_limit_bytes=48 * MIB),
        cost_estimate=SLIGHT,
        name="project",
    )(x, gain, weights)


def split_store(core_ref, value, keep_ref, send_ref):
    parts = keep_ref.shape[:-2]
    half = keep_ref.shape[-2]
    value = value.astype(BF16).reshape(parts + (2, half, WIDTH))
    lower = value[..., 0, :, :]
    upper = value[..., 1, :, :]
    first = core_ref[0] == 0
    keep_ref[...] = jnp.where(first, lower, upper)
    send_ref[...] = jnp.where(first, upper, lower)


def weight_grads_kernel(core_ref, d_ref, dml_ref, a1_ref, o_ref, *refs):
    keep_ref, send_ref, a1t_ref = refs[-3:]
    step = pl.program_id(0)

    @pl.when(step == 0)
    def _():
        split_store(core_ref, mm_tn(o_ref[...], dml_ref[...]), keep_ref, send_ref)
        a1t_ref[...] = a1_ref[...].T

    @pl.when(step > 0)
    def _():
        split_store(core_ref, mm(a1t_ref[...], d_ref[0]), keep_ref, send_ref)


def weight_grads(core, dqkv, dml, a1, o, parts, after=()):
    rows = a1.shape[0]
    half = WIDTH // parts // 2
    whole = lambda shape: pl.BlockSpec(shape, lambda k: (0,) * len(shape), pipeline_mode=pl.Buffered(1))
    block = pl.BlockSpec((parts, 1, half, WIDTH), lambda k: (0, lax.rem(k + 3, 4), 0, 0))
    out = jax.ShapeDtypeStruct((parts, 4, half, WIDTH), BF16)
    return pl.pallas_call(
        weight_grads_kernel,
        grid=(4,),
        in_specs=[
            pl.BlockSpec(memory_space=pltpu.SMEM),
            pl.BlockSpec((1, rows, WIDTH), lambda k: (jnp.maximum(k - 1, 0), 0, 0)),
            whole((rows, WIDTH)),
            whole((rows, WIDTH)),
            whole((rows, WIDTH)),
        ]
        + [pl.BlockSpec(memory_space=pl.ANY)] * len(after),
        out_specs=[block, block],
        out_shape=[out, out],
        scratch_shapes=[pltpu.VMEM((WIDTH, rows), BF16)],
        compiler_params=pltpu.CompilerParams(vmem_limit_bytes=48 * MIB),
        cost_estimate=SLIGHT,
        name="weight_grads",
    )(core, dqkv, dml, a1, o, *after)


def input_grad_kernel(d_ref, x_ref, gain_ref, dmid_ref, w_ref, *refs):
    gin_ref, gg_ref, acc_ref = refs[-3:]
    step = pl.program_id(0)

    @pl.when(step == 0)
    def _():
        acc_ref[...] = jnp.zeros_like(acc_ref)

    acc_ref[...] += mm_nt(d_ref[0], square(w_ref))

    @pl.when(step == 2)
    def _():
        x = x_ref[...].astype(F32)
        dx, dg = norm_back(x, gain_ref[...], acc_ref[...])
        gin_ref[...] = (dmid_ref[...] + dx).astype(BF16)
        gg_ref[...] = dg


def input_grad(dqkv, x, gain, dmid, weights, after=()):
    rows = x.shape[0]
    parts, _, per, _ = weights.shape
    whole = lambda shape: pl.BlockSpec(shape, lambda k: (0,) * len(shape), pipeline_mode=pl.Buffered(1))
    return pl.pallas_call(
        input_grad_kernel,
        grid=(3,),
        in_specs=[
            pl.BlockSpec((1, rows, WIDTH), lambda k: (k, 0, 0)),
            whole((rows, WIDTH)),
            whole((1, WIDTH)),
            whole((rows, WIDTH)),
            pl.BlockSpec((parts, 1, per, WIDTH), lambda k: (0, k, 0, 0)),
        ]
        + [pl.BlockSpec(memory_space=pl.ANY)] * len(after),
        out_specs=[whole((rows, WIDTH)), whole((1, WIDTH))],
        out_shape=[
            jax.ShapeDtypeStruct((rows, WIDTH), BF16),
            jax.ShapeDtypeStruct((1, WIDTH), F32),
        ],
        scratch_shapes=[pltpu.VMEM((rows, WIDTH), F32)],
        compiler_params=pltpu.CompilerParams(vmem_limit_bytes=48 * MIB),
        cost_estimate=SLIGHT,
        name="input_grad",
    )(dqkv, x, gain, dmid, weights, *after)


def attend_kernel(off_ref, labj_ref, labi_ref, q_ref, k_ref, v_ref, o_ref, p_ref, band_ref):
    @pl.when(pl.program_id(1) == 0)
    def _():
        for head in range(2):
            row = jnp.broadcast_to(off_ref[0, head : head + 1, :], (LANES, OFFS))
            band_ref[head] = pltpu.roll(row, 0, 1, stride=1, stride_axis=0)

    q = q_ref[0, 0]
    k = k_ref[0, 0]
    vt = v_ref[0, 0].T
    span = 2 * LANES
    for head in range(2):
        km = half_lanes(k, head)
        vth = vt[head * HD : (head + 1) * HD]
        for part in range(ROWS // span):
            at = part * span
            scores = mm_nt(km, q[at : at + span])
            tiles = []
            for c in range(ROWS // LANES):
                lo = BAND - LANES * c + at
                same = labj_ref[0, c * LANES : (c + 1) * LANES, :] == labi_ref[0, 0:1, at : at + span]
                tiles.append(
                    jnp.where(
                        same,
                        scores[c * LANES : (c + 1) * LANES] + band_ref[head, :, lo : lo + span],
                        MASKED,
                    )
                )
            scores = jnp.concatenate(tiles, axis=0)
            peak = jnp.max(scores, axis=0, keepdims=True)
            powers = jnp.exp(scores - peak)
            scale = 1.0 / jnp.sum(powers, axis=0, keepdims=True)
            probs = (powers * scale).astype(BF16)
            p_ref[0, 0, head, :, at : at + span] = probs
            mixed = mm(vth, probs)
            o_ref[0, at : at + span, head * HD : (head + 1) * HD] = mixed.T.astype(BF16)


def attend(off_rows, lab_keys, lab_queries, qkv):
    blocks = qkv.shape[1]
    return pl.pallas_call(
        attend_kernel,
        grid=(PAIRS, blocks),
        in_specs=[
            pl.BlockSpec((1, 2, OFFS), lambda p, b: (p, 0, 0)),
            pl.BlockSpec((1, ROWS, 1), lambda p, b: (b, 0, 0)),
            pl.BlockSpec((1, 8, ROWS), lambda p, b: (b, 0, 0)),
            pl.BlockSpec((1, 1, ROWS, LANES), lambda p, b: (0, b, 0, p)),
            pl.BlockSpec((1, 1, ROWS, LANES), lambda p, b: (1, b, 0, p)),
            pl.BlockSpec((1, 1, ROWS, LANES), lambda p, b: (2, b, 0, p)),
        ],
        out_specs=[
            pl.BlockSpec((1, ROWS, LANES), lambda p, b: (b, 0, p)),
            pl.BlockSpec((1, 1, 2, ROWS, ROWS), lambda p, b: (p, b, 0, 0, 0)),
        ],
        out_shape=[
            jax.ShapeDtypeStruct((blocks, ROWS, WIDTH), BF16),
            jax.ShapeDtypeStruct((PAIRS, blocks, 2, ROWS, ROWS), BF16),
        ],
        scratch_shapes=[pltpu.VMEM((2, LANES, OFFS), F32)],
        compiler_params=pltpu.CompilerParams(vmem_limit_bytes=48 * MIB),
        cost_estimate=SLIGHT,
        name="attend",
    )(off_rows, lab_keys, lab_queries, qkv, qkv, qkv)


def attend_back_kernel(q_ref, k_ref, v_ref, do_ref, p_ref, *refs):
    d_ref, gt_ref, band_ref = refs[-3:]
    block = pl.program_id(1)

    @pl.when(block == 0)
    def _():
        band_ref[...] = jnp.zeros_like(band_ref)

    q = q_ref[0, 0]
    k = k_ref[0, 0]
    v = v_ref[0, 0]
    do = do_ref[0]
    kt = k.T
    dk = None
    dv = None
    for head in range(2):
        vm = half_lanes(v, head)
        probs_low = p_ref[0, 0, head]
        probs = probs_low.astype(F32)
        weighted = probs * mm_nt(vm, do)
        total = jnp.sum(weighted, axis=0, keepdims=True)
        ds = weighted - probs * total
        for tile in range(7):
            add = None
            for c in range(4):
                i = tile - 3 + c
                if 0 <= i < 4:
                    part = ds[c * LANES : (c + 1) * LANES, i * LANES : (i + 1) * LANES]
                    add = part if add is None else add + part
            band_ref[head, :, tile * LANES : (tile + 1) * LANES] += add
        ds = ds.astype(BF16)
        dv_part = mm(probs_low, half_lanes(do, head))
        dk_part = mm(ds, half_lanes(q, head))
        dv = dv_part if dv is None else dv + dv_part
        dk = dk_part if dk is None else dk + dk_part
        dq = mm(kt[head * HD : (head + 1) * HD], ds)
        d_ref[0, 0, :, head * HD : (head + 1) * HD] = dq.T.astype(BF16)
    d_ref[1, 0] = dk.astype(BF16)
    d_ref[2, 0] = dv.astype(BF16)

    @pl.when(block == pl.num_programs(1) - 1)
    def _():
        for head in range(2):
            folded = band_ref[head]
            size = LANES // 2
            while size >= 8:
                folded = folded[:size] + pltpu.roll(folded[size : 2 * size], OFFS - size, 1)
                size //= 2
            row = lax.broadcasted_iota(jnp.int32, (8, OFFS), 0)
            for bit in (4, 2, 1):
                folded = jnp.where((row & bit) != 0, pltpu.roll(folded, OFFS - bit, 1), folded)
            gt_ref[0, head : head + 1, :] = jnp.sum(folded, axis=0, keepdims=True)


def attend_back(qkv, do, probs, first, count, before=None, after=()):
    blocks = qkv.shape[1]
    extra = (() if before is None else (before,)) + tuple(after)
    return pl.pallas_call(
        attend_back_kernel,
        grid=(count, blocks),
        in_specs=[
            pl.BlockSpec((1, 1, ROWS, LANES), lambda p, b: (0, b, 0, p + first)),
            pl.BlockSpec((1, 1, ROWS, LANES), lambda p, b: (1, b, 0, p + first)),
            pl.BlockSpec((1, 1, ROWS, LANES), lambda p, b: (2, b, 0, p + first)),
            pl.BlockSpec((1, ROWS, LANES), lambda p, b: (b, 0, p + first)),
            pl.BlockSpec((1, 1, 2, ROWS, ROWS), lambda p, b: (p + first, b, 0, 0, 0)),
        ]
        + [pl.BlockSpec(memory_space=pl.ANY)] * len(extra),
        out_specs=[
            pl.BlockSpec((3, 1, ROWS, LANES), lambda p, b: (0, b, 0, p + first)),
            pl.BlockSpec((1, 2, OFFS), lambda p, b: (p, 0, 0)),
        ],
        out_shape=[
            jax.ShapeDtypeStruct((3, blocks, ROWS, WIDTH), BF16),
            jax.ShapeDtypeStruct((count, 2, OFFS), F32),
        ],
        input_output_aliases={} if before is None else {5: 0},
        scratch_shapes=[pltpu.VMEM((2, LANES, OFFS), F32)],
        compiler_params=pltpu.CompilerParams(vmem_limit_bytes=48 * MIB),
        cost_estimate=SLIGHT,
        name="attend_back",
    )(qkv, qkv, qkv, do, probs, *extra)


def gelu_pair(u):
    c = 0.7978845608028654
    sq = u * u
    th = jnp.tanh(u * (c + (c * 0.044715) * sq))
    half = 0.5 * th + 0.5
    slope = half + (0.5 * u) * (1.0 - th * th) * (c + (3.0 * c * 0.044715) * sq)
    return u * half, slope


def feed_kernel(core_ref, x_ref, o_ref, dyl_ref, gain_ref, wo_ref, wi_ref, wf_ref,
                out_ref, dmid_ref, do_ref, dml_ref, wi_keep, wi_send, wf_keep, wf_send, gg_ref,
                mid_ref, a2_ref, a2t_ref, acc_ref, f_ref, du_ref):
    step = pl.program_id(0)
    rows = x_ref.shape[0]
    chunk = ROWS

    @pl.when(step == 0)
    def _():
        wo = square(wo_ref)
        for at in range(0, rows, chunk):
            here = pl.ds(at, chunk)
            mid = x_ref[here].astype(F32) + mm(o_ref[here], wo)
            mid_ref[here] = mid
            a2_ref[here] = (mid * inverse_rms(mid) * gain_ref[...]).astype(BF16)
            acc_ref[here] = mid
            dmid_ref[here] = jnp.zeros((chunk, WIDTH), F32)
        a2t_ref[...] = a2_ref[...].T

    wi = square(wi_ref)
    wf = square(wf_ref)
    for at in range(0, rows, chunk):
        here = pl.ds(at, chunk)
        u = mm(a2_ref[here], wi)
        da = mm_nt(dyl_ref[here], wf)
        f, slope = gelu_pair(u)
        f = f.astype(BF16)
        du = (da * slope).astype(BF16)
        f_ref[here] = f
        du_ref[here] = du
        acc_ref[here] += mm(f, wf)
        dmid_ref[here] += mm_nt(du, wi)
    split_store(core_ref, mm_tn(f_ref[...], dyl_ref[...]), wf_keep, wf_send)
    split_store(core_ref, mm(a2t_ref[...], du_ref[...]), wi_keep, wi_send)

    @pl.when(step == pl.num_programs(0) - 1)
    def _():
        gg = jnp.zeros((1, WIDTH), F32)
        wo = square(wo_ref)
        for at in range(0, rows, chunk):
            here = pl.ds(at, chunk)
            out_ref[here] = acc_ref[here].astype(BF16)
            dm, dg = norm_back(mid_ref[here], gain_ref[...], dmid_ref[here])
            gg += dg
            dm = dm + dyl_ref[here].astype(F32)
            dmid_ref[here] = dm
            low = dm.astype(BF16)
            dml_ref[here] = low
            do_ref[here] = mm_nt(low, wo).astype(BF16)
        gg_ref[...] = gg


def feed(core, x, o, dyl, gain, rest):
    rows = x.shape[0]
    parts, _, per, _ = rest.shape
    group = WIDTH // (4 * per) if parts > 1 else 1
    wf_map = (lambda t: (t, 0, 0, 0)) if parts > 1 else (lambda t: (0, t, 0, 0))
    wf_block = (group, 4, per, WIDTH) if parts > 1 else (1, 1, per, WIDTH)
    half = per // 2
    wf_half = pl.BlockSpec(wf_block[:2] + (half, WIDTH), wf_map)
    wi_half = pl.BlockSpec((parts, 1, half, WIDTH), lambda t: (0, t, 0, 0))
    halves = jax.ShapeDtypeStruct((parts, 4, half, WIDTH), BF16)
    one = (parts, 1, per, WIDTH)
    whole = lambda shape: pl.BlockSpec(shape, lambda t: (0,) * len(shape), pipeline_mode=pl.Buffered(1))
    full = (rows, WIDTH)
    return pl.pallas_call(
        feed_kernel,
        grid=(FF // WIDTH,),
        in_specs=[
            pl.BlockSpec(memory_space=pltpu.SMEM),
            whole(full),
            whole(full),
            whole(full),
            whole((1, WIDTH)),
            pl.BlockSpec(one, lambda t: (0, 8, 0, 0), pipeline_mode=pl.Buffered(1)),
            pl.BlockSpec(one, lambda t: (0, 4 + t, 0, 0)),
            pl.BlockSpec(wf_block, wf_map),
        ],
        out_specs=[
            whole(full),
            whole(full),
            whole(full),
            whole(full),
            wi_half,
            wi_half,
            wf_half,
            wf_half,
            whole((1, WIDTH)),
        ],
        out_shape=[
            jax.ShapeDtypeStruct(full, BF16),
            jax.ShapeDtypeStruct(full, F32),
            jax.ShapeDtypeStruct(full, BF16),
            jax.ShapeDtypeStruct(full, BF16),
            halves,
            halves,
            halves,
            halves,
            jax.ShapeDtypeStruct((1, WIDTH), F32),
        ],
        scratch_shapes=[
            pltpu.VMEM(full, F32),
            pltpu.VMEM(full, BF16),
            pltpu.VMEM((WIDTH, rows), BF16),
            pltpu.VMEM(full, F32),
            pltpu.VMEM(full, BF16),
            pltpu.VMEM(full, BF16),
        ],
        compiler_params=pltpu.CompilerParams(vmem_limit_bytes=60 * MIB),
        cost_estimate=SLIGHT,
        name="feed",
    )(core, x, o, dyl, gain, rest, rest, rest)


class Links:
    def __init__(self):
        dp, fsdp = lax.axis_index("dp"), lax.axis_index("fsdp")
        self.core, self.y = dp % 2, dp // 2
        self.x, self.z = fsdp % 2, fsdp // 2

    def swap(self, value, core=0, y=0, x=0, z=0):
        dp_bits, fsdp_bits = 2 * y + core, 2 * z + x
        pairs = [
            (8 * d + f, 8 * (d ^ dp_bits) + (f ^ fsdp_bits)) for d in range(4) for f in range(8)
        ]
        return lax.ppermute(value, ("dp", "fsdp"), pairs)


def place_kernel(at_ref, *refs):
    pieces, out_ref = refs[:-1], refs[-1]
    for n, piece in enumerate(pieces):
        for slot in range(4):
            spot = 3 * (4 * n + slot)
            out_ref[at_ref[spot], at_ref[spot + 1], at_ref[spot + 2]] = piece[slot]


def place(at, pieces, parts, kinds):
    half = pieces[0].shape[1]
    out = pl.pallas_call(
        place_kernel,
        in_specs=[pl.BlockSpec(memory_space=pltpu.SMEM)]
        + [pl.BlockSpec(memory_space=pltpu.VMEM)] * len(pieces),
        out_specs=pl.BlockSpec(memory_space=pltpu.VMEM),
        out_shape=jax.ShapeDtypeStruct((parts, kinds, 2, half, WIDTH), BF16),
        compiler_params=pltpu.CompilerParams(vmem_limit_bytes=24 * MIB),
        name="place",
    )(at, *pieces)
    return out.reshape(parts, kinds, 2 * half, WIDTH)


def fetch_weights(links, shard):
    half = shard.shape[1] // 2
    mine = lax.dynamic_slice_in_dim(shard, links.core * half, half, axis=1)
    both = mine[0]
    one = lax.dynamic_index_in_dim(mine, 1 + links.y, 0, keepdims=False)
    first = jnp.stack([both, one])
    level = jnp.stack([first, links.swap(first, z=2)], axis=1)
    more = links.swap(level, z=1)
    level_a = jnp.concatenate([level[1], more[1]])
    level_b = jnp.concatenate([level[0], more[0]])
    across_a = links.swap(level_a, x=1)
    over_a = links.swap(level_a, y=1)
    across_b = links.swap(level_b, x=1)
    over_across = links.swap(across_a, y=1)
    pieces, at = [], []
    for value, kind, x_bit in (
        (level_a, 1 + links.y, 0),
        (level_b, 0, 0),
        (across_a, 1 + links.y, 1),
        (over_a, 2 - links.y, 0),
        (across_b, 0, 1),
        (over_across, 2 - links.y, 1),
    ):
        for piece, core in ((value, links.core), (links.swap(value, core=1), 1 - links.core)):
            pieces.append(piece)
            for slot in range(4):
                z = links.z ^ ((slot % 2) * 2 + slot // 2)
                at += [2 * z + (links.x ^ x_bit), kind, core]
    at = jnp.stack([jnp.asarray(v, jnp.int32) for v in at])
    return place(at, pieces, 8, 3)


def pick(value, index, axis):
    return lax.dynamic_index_in_dim(value, index, axis, keepdims=False)


def added(a, b):
    return a.astype(F32) + b.astype(F32)


def by_x(value):
    return value.reshape((4, 2) + value.shape[1:])


def lanes(value, which):
    cut = WIDTH // 2
    return lax.dynamic_slice_in_dim(value, which * cut, cut, axis=value.ndim - 1)


class GradSum:
    def __init__(self, links, keep_a, send_a, keep_b, send_b):
        self.links = links
        self.a, self.b = keep_a, keep_b
        self.sent = (send_a, send_b)
        self.got = tuple(links.swap(v, core=1) for v in self.sent)

    def wait(self, *others):
        self.got = tuple(lax.optimization_barrier(self.got + others))[: len(self.got)]

    def first(self):
        links, a, b = self.links, self.a, self.b
        got_a, got_b = self.got
        go_a = added(lanes(a, 1 - links.y), lanes(got_a, 1 - links.y)).astype(BF16)
        go_b = added(pick(by_x(b), 1 - links.x, 1), pick(by_x(got_b), 1 - links.x, 1)).astype(BF16)
        self.sent = (go_a, go_b)
        self.got = (links.swap(go_a, y=1), links.swap(go_b, x=1))
        self.a = added(lanes(a, links.y), lanes(got_a, links.y)).astype(BF16)
        self.b = added(pick(by_x(b), links.x, 1), pick(by_x(got_b), links.x, 1)).astype(BF16)

    def second(self):
        links, a, b = self.links, self.a, self.b
        got_a, got_b = self.got
        go_a = added(pick(by_x(a), 1 - links.x, 1), pick(by_x(got_a), 1 - links.x, 1)).astype(BF16)
        go_b = added(lanes(b, 1 - links.y), lanes(got_b, 1 - links.y)).astype(BF16)
        self.sent = (go_a, go_b)
        self.got = (links.swap(go_a, x=1), links.swap(go_b, y=1))
        self.a = added(pick(by_x(a), links.x, 1), pick(by_x(got_a), links.x, 1)).astype(BF16)
        self.b = added(lanes(b, links.y), lanes(got_b, links.y)).astype(BF16)

    def third(self):
        links = self.links
        got_a, got_b = self.got

        def at_z(z):
            a = added(pick(self.a, z, 0), pick(got_a, z, 0))
            b = added(pick(self.b, z, 0), pick(got_b, z, 0))
            return jnp.concatenate([a, b])

        self.sent = tuple(at_z(links.z ^ bits).astype(BF16) for bits in (2, 3, 1))
        self.got = tuple(links.swap(v, z=bits) for v, bits in zip(self.sent, (2, 3, 1)))
        self.total = at_z(links.z)

    def third_by_collective(self):
        got_a, got_b = self.got
        total = jnp.concatenate([added(self.a, got_a), added(self.b, got_b)], axis=1).astype(BF16)
        kinds, half, cut = total.shape[1:]
        self.total = total
        groups = [[2 * z + x for z in range(4)] for x in range(2)]
        self.mine = lax.psum_scatter(
            total.reshape(-1, cut), "fsdp", scatter_dimension=0, tiled=True, axis_index_groups=groups
        )

    def gather(self, *others):
        mine = tie(self.mine, *others)
        return lax.all_gather(mine, "dp", axis=0, tiled=True).reshape((4,) + self.total.shape[1:])

    def sum_up(self):
        total = self.total
        for part in self.got:
            total = total + part.astype(F32)
        self.total = total.astype(BF16)

    def last(self):
        links = self.links
        total = self.total
        other = links.swap(total, y=1)
        left = jnp.where(links.y == 0, total, other)
        right = jnp.where(links.y == 0, other, total)
        mine = jnp.concatenate([left, right], axis=-1)
        return mine, links.swap(mine, core=1)


def tie(value, *others):
    return lax.optimization_barrier((value,) + others)[0]


def sum_small(links, value, steps, marks=()):
    for n, step in enumerate(steps):
        if n < len(marks):
            value = tie(value, *marks[n])
        value = value + links.swap(value, **step)
    return value


FSDP_STEPS = (dict(z=2), dict(z=1), dict(x=1))
ALL_STEPS = (dict(core=1), dict(x=1), dict(y=1), dict(z=2), dict(z=1))


def moments(weight, first, second, grad):
    first_new = BETA_ONE * first + (1.0 - BETA_ONE) * grad
    second_new = BETA_TWO * second + (1.0 - BETA_TWO) * grad * grad
    root = jnp.sqrt(second_new * (1.0 / (1.0 - BETA_TWO**STEP)))
    direction = first_new * (1.0 / (1.0 - BETA_ONE**STEP)) / (root + ADAM_EPS) + DECAY * weight
    return (first_new, second_new, direction)


def update_kernel(count, core_ref, *refs):
    grad_refs, (p_ref, m_ref, v_ref), outs = refs[:count], refs[count : count + 3], refs[count + 3 :]
    m_out, v_out, r_out, sum_out = outs[0], outs[1], outs[-2], outs[-1]
    half = grad_refs[0].shape[-2]
    if count == 1:
        pieces = [grad_refs[0][n, 0].astype(F32) for n in range(4)]
        grads = [jnp.concatenate([pieces[core], pieces[2 + core]], axis=1) for core in range(2)]
    else:
        first = core_ref[0] == 0
        mine, theirs = (ref[...].reshape(half, WIDTH).astype(F32) for ref in grad_refs)
        grads = [jnp.where(first, mine, theirs), jnp.where(first, theirs, mine)]
    squares = [jnp.zeros((1, WIDTH), F32)] * 2
    flat = lambda ref: ref.at[0] if len(ref.shape) == 3 else ref
    p_ref, m_ref, v_ref, m_out, r_out = (flat(ref) for ref in (p_ref, m_ref, v_ref, m_out, r_out))
    for part in range(2):
        here = pl.ds(part * half, half)
        grad = grads[part]
        weight = p_ref[here]
        m_new, v_new, r = moments(weight, m_ref[here], v_ref[here], grad)
        m_out[here] = m_new
        r_out[here] = r
        if len(outs) == 4:
            v_out[here] = v_new
        else:

            @pl.when(pl.program_id(0) < 3)
            def _():
                v_out[0, here] = v_new

            @pl.when(pl.program_id(0) == 3)
            def _():
                outs[2][here] = v_new

        squares[0] += jnp.sum(weight * weight, axis=0, keepdims=True)
        squares[1] += jnp.sum(r * r, axis=0, keepdims=True)
    sum_out[0] = jnp.concatenate(squares, axis=0)


def update(core, grads, start, arrays, by_lanes=False):
    weight = arrays[0]
    half = grads[0].shape[-2]
    per = 2 * half
    stacked = weight.ndim == 3
    if stacked:
        block = pl.BlockSpec((1, per, WIDTH), lambda k: (k, 0, 0))
        v_specs = [
            pl.BlockSpec((1, per, WIDTH), lambda k: (jnp.minimum(k, 2), 0, 0)),
            pl.BlockSpec((per, WIDTH), lambda k: (0, 0)),
        ]
        v_shapes = [
            jax.ShapeDtypeStruct((3, per, WIDTH), F32),
            jax.ShapeDtypeStruct((per, WIDTH), F32),
        ]
    else:
        block = pl.BlockSpec((per, WIDTH), (lambda k: (0, k)) if by_lanes else (lambda k: (k, 0)))
        v_specs = [block]
        v_shapes = [jax.ShapeDtypeStruct(weight.shape, F32)]
    if len(grads) == 1:
        grad_spec = pl.BlockSpec((4, 1, half, WIDTH // 2), lambda k: (0, k + start, 0, 0))
    else:
        grad_spec = pl.BlockSpec((1, half, WIDTH), lambda k: (k + start, 0, 0))
    like = jax.ShapeDtypeStruct(weight.shape, F32)
    return pl.pallas_call(
        functools.partial(update_kernel, len(grads)),
        grid=(4,),
        in_specs=[pl.BlockSpec(memory_space=pltpu.SMEM)] + [grad_spec] * len(grads) + [block] * 3,
        out_specs=[block] + v_specs + [block, pl.BlockSpec((1, 2, WIDTH), lambda k: (k, 0, 0))],
        out_shape=[like] + v_shapes + [like, jax.ShapeDtypeStruct((4, 2, WIDTH), F32)],
        compiler_params=pltpu.CompilerParams(vmem_limit_bytes=60 * MIB),
        cost_estimate=SLIGHT,
        name="update",
    )(core, *grads, *arrays)


def row_labels(lengths):
    ends = jnp.cumsum(lengths, axis=1)
    places = jnp.arange(ROWS, dtype=jnp.int32)
    labels = jnp.sum((places[None, :, None] >= ends[:, None, :]).astype(jnp.int32), axis=2)
    return labels, places[None, :] < ends[:, -1:]


def body(
    tokens, cotangent, seg_lengths, bucket_of,
    attn_w, attn_m, attn_v, ffin_w, ffin_m, ffin_v, ffout_w, ffout_m, ffout_v,
    gains, gains_m, gains_v, table, table_m, table_v,
):
    fsdp = lax.axis_size("fsdp")
    dp = lax.axis_size("dp")
    both = ("fsdp", "dp")
    batches, count, width = tokens.shape
    rows = batches * count
    blocks = rows // ROWS
    per = attn_w.shape[1]
    direct = per % 32 == 0
    paired = direct and fsdp == 8 and dp == 4
    links = Links() if paired else None
    core = (links.core if paired else jnp.int32(0)).reshape(1)

    me = lax.axis_index("dp")

    def spread(shard):
        flat = shard.reshape(-1, WIDTH)
        size = flat.shape[0] // dp
        mine = lax.dynamic_slice_in_dim(flat, me * size, size, axis=0)
        return lax.all_gather(mine, both, axis=0, tiled=True).reshape((fsdp,) + shard.shape)

    def whole_of(gathered):
        kinds = gathered.shape[1]
        return gathered.transpose(1, 0, 2, 3).reshape(1, kinds, WIDTH, WIDTH)

    attn_low = attn_w.astype(BF16)
    ffin_low = ffin_w.astype(BF16).reshape(per, 4, WIDTH).transpose(1, 0, 2)
    ffout_low = ffout_w.astype(BF16).reshape(4, per, WIDTH)
    qkv_w = fetch_weights(links, attn_low[:3]) if paired else spread(attn_low[:3])
    rest_w = spread(jnp.concatenate([ffout_low, ffin_low, attn_low[3:]], axis=0))
    if not direct:
        qkv_w = whole_of(qkv_w)
        wf_all = rest_w[:, :4].reshape(1, 4, WIDTH, WIDTH)
        rest_w = jnp.concatenate([wf_all, whole_of(rest_w[:, 4:])], axis=1)
    small = jnp.concatenate([gains.reshape(-1), table.reshape(-1)]).astype(BF16)
    if paired:
        own = jnp.arange(fsdp)[:, None] == lax.axis_index("fsdp")
        small = sum_small(links, jnp.where(own, small[None].astype(F32), 0.0), FSDP_STEPS).astype(BF16)
    else:
        small = lax.all_gather(small, "fsdp", axis=0)
    gain_full = small[:, : 2 * per].reshape(fsdp, 2, per).transpose(1, 0, 2).reshape(2, 1, width).astype(F32)
    table_full = small[:, 2 * per :].reshape(BUCKETS, HEADS)

    padded = jnp.concatenate([bucket_of, jnp.full((1,), -1, jnp.int32)])
    padded = jnp.roll(padded[::-1], -(OFFS - 1 - 7 * LANES + 1))
    onehot = (padded[None, :] == jnp.arange(BUCKETS, dtype=jnp.int32)[:, None]).astype(BF16)
    off_rows = lax.dot_general(
        table_full, onehot, (((0,), (0,)), ((), ())), preferred_element_type=F32
    ).reshape(PAIRS, 2, OFFS)

    labels, valid = row_labels(seg_lengths.reshape(blocks, -1))
    lab_keys = labels[:, :, None]
    lab_queries = jnp.broadcast_to(labels[:, None, :], (blocks, 8, ROWS))
    x = tokens.reshape(rows, width)
    dyl = jnp.where(valid.reshape(rows, 1), cotangent.reshape(rows, width), jnp.zeros((), BF16))

    qkv, a1 = project(x, gain_full[0], qkv_w)
    qkv = qkv.reshape(3, blocks, ROWS, width)
    o, probs = attend(off_rows, lab_keys, lab_queries, qkv)
    out, dmid, do, dml, wi_keep, wi_send, wf_keep, wf_send, gg2 = feed(
        core, x, o.reshape(rows, width), dyl, gain_full[1], rest_w
    )
    do = do.reshape(blocks, ROWS, width)
    o = o.reshape(rows, width)
    parts = qkv_w.shape[0]
    if paired:
        feed_sum = GradSum(links, wf_keep, wf_send, wi_keep, wi_send)
        dqkv, gt0 = attend_back(qkv, do, probs, 0, 2)
        feed_sum.wait(gt0)
        feed_sum.first()
        dqkv, gt1 = attend_back(qkv, do, probs, 2, 2, dqkv, feed_sum.sent)
        dqkv, gt2 = attend_back(qkv, do, probs, 4, 2, dqkv)
        dqkv = dqkv.reshape(3, rows, width)
        feed_sum.wait(gt2)
        feed_sum.second()
        keep, send = weight_grads(core, dqkv, dml, a1, o, parts, feed_sum.sent)
        feed_sum.wait(keep)
        feed_sum.third_by_collective()
        send = tie(send, feed_sum.total)
        attn_sum = GradSum(links, keep[:, :2], send[:, :2], keep[:, 2:], send[:, 2:])
        attn_sum.first()
        gin, gg1 = input_grad(dqkv, x, gain_full[0], dmid, qkv_w, attn_sum.sent)
        attn_sum.wait(gg1)
        attn_sum.second()
        marks = [attn_sum.sent]
        attn_sum.third()
        marks += [attn_sum.sent] * 2
        feed_grads = feed_sum.gather(*attn_sum.sent)
        attn_sum.sum_up()
        feed_grads = (tie(feed_grads, attn_sum.total),)
        gt = jnp.concatenate([gt0, gt1, gt2])
    else:
        dqkv, gt = attend_back(qkv, do, probs, 0, PAIRS)
        dqkv = dqkv.reshape(3, rows, width)
        keep, send = weight_grads(core, dqkv, dml, a1, o, parts)
        gin, gg1 = input_grad(dqkv, x, gain_full[0], dmid, qkv_w)
    grad_table = lax.dot_general(
        onehot.astype(F32), gt.reshape(HEADS, OFFS), (((1,), (1,)), ((), ())),
        preferred_element_type=F32, precision=lax.Precision.HIGHEST,
    )

    def parts_of(grad):
        kinds = grad.shape[1]
        return grad.reshape(kinds, fsdp, per, WIDTH).transpose(1, 0, 2, 3)

    def gather_sum(grad):
        kinds = grad.shape[1]
        flat = grad.reshape(fsdp * kinds * per, WIDTH)
        mine = lax.psum_scatter(flat, both, scatter_dimension=0, tiled=True)
        return lax.all_gather(mine, "dp", axis=0, tiled=True).reshape(kinds, per, WIDTH).astype(F32)

    if not paired:
        dwf = jnp.concatenate([wf_keep, wf_send], axis=2).reshape(fsdp, 4, per, WIDTH)
        dwi = jnp.concatenate([wi_keep, wi_send], axis=2)
        dw = jnp.concatenate([keep, send], axis=2)
        if not direct:
            dwi, dw = parts_of(dwi), parts_of(dw)
        halves = lambda v: (v[:, : per // 2], v[:, per // 2 :])
        feed_grads = halves(gather_sum(jnp.concatenate([dwf, dwi], axis=1)))
        attn_mine, attn_theirs = halves(gather_sum(dw))
        marks = []

    grad_gains = jnp.concatenate([gg1, gg2], axis=0).reshape(2, fsdp, per).transpose(1, 0, 2).reshape(fsdp, -1)
    grad_small = jnp.concatenate([grad_gains, grad_table.reshape(fsdp, -1)], axis=1)
    out_m, out_v, out_r, out_sq = update(core, feed_grads, 0, (ffout_w, ffout_m, ffout_v))
    in_m, in_v, in_r, in_sq = update(core, feed_grads, 4, (ffin_w, ffin_m, ffin_v), True)
    feed_sq = jnp.stack([jnp.sum(in_sq, axis=(0, 2)), jnp.sum(out_sq, axis=(0, 2))], axis=1)
    if paired:
        attn_mine, attn_theirs = attn_sum.last()
        marks += [(attn_sum.total,)]
        grad_small = sum_small(links, grad_small, ALL_STEPS, marks)
    else:
        grad_small = lax.psum(grad_small, ("dp", "fsdp"))
    grad_small = lax.dynamic_index_in_dim(grad_small, lax.axis_index("fsdp"), 0, keepdims=False)

    flat = lambda a, b: jnp.concatenate([a.reshape(-1), b.reshape(-1)])
    small_p = flat(gains, table)
    small_m, small_v, small_r = moments(small_p, flat(gains_m, table_m), flat(gains_v, table_v), grad_small)
    kind = jnp.minimum(jnp.arange(small_p.shape[0]) // per, 2)
    member = kind[None, :] == jnp.arange(3)[:, None]
    squares = lambda v: jnp.sum(jnp.where(member, (v * v)[None], 0.0), axis=1)

    attn_new_m, attn_new_v, out_new_v, attn_r, attn_sq = update(
        core, (attn_mine, attn_theirs), 0, (attn_w, attn_m, attn_v)
    )
    attn_sq = jnp.sum(attn_sq, axis=2).T
    sums = jnp.concatenate([attn_sq, feed_sq, jnp.stack([squares(small_p), squares(small_r)])], axis=1)
    sums = sum_small(links, sums, FSDP_STEPS) if paired else lax.psum(sums, "fsdp")
    weight_norms, step_norms = jnp.sqrt(sums[0]), jnp.sqrt(sums[1])
    scale = RATE * (weight_norms / (step_norms + ADAM_EPS))
    attn_new = attn_w - scale[:4][:, None, None] * attn_r
    ffin_new = ffin_w - scale[4] * in_r
    ffout_new = ffout_w - scale[5] * out_r
    small_new = small_p - jnp.sum(jnp.where(member, scale[6:][:, None], 0.0), axis=0) * small_r

    def unpack(v):
        return v[: 2 * per].reshape(2, per), v[2 * per :].reshape(table.shape)

    gains_new, table_new = unpack(small_new)
    gains_m_new, table_m_new = unpack(small_m)
    gains_v_new, table_v_new = unpack(small_v)
    norms = jnp.stack([weight_norms, step_norms], axis=1)
    return (
        out.reshape(tokens.shape),
        gin.reshape(tokens.shape),
        attn_new, attn_new_m, attn_new_v, out_new_v,
        ffin_new, in_m, in_v,
        ffout_new, out_m, out_v,
        gains_new, gains_m_new, gains_v_new,
        table_new, table_m_new, table_v_new,
        norms,
    )


def solution(mesh):
    batch = P(None, ("dp", "fsdp"), None)
    mid_dim = P(None, "fsdp", None)
    first = P("fsdp", None)
    last = P(None, "fsdp")
    in_specs = (batch, batch, batch, P()) + (mid_dim,) * 3 + (first,) * 6 + (last,) * 3 + (first,) * 3
    out_specs = (batch, batch) + (mid_dim,) * 3 + (first,) * 7 + (last,) * 3 + (first,) * 3 + (P(),)
    return jax.shard_map(body, mesh=mesh, in_specs=in_specs, out_specs=out_specs, check_vma=False)
```

```python
import jax
import jax.numpy as jnp
from jax import lax
from jax.experimental import pallas as pl
from jax.experimental.pallas import tpu as pltpu
from jax.sharding import PartitionSpec as P

HEADS = 12
HD = 64
BUCKETS = 32
ROWS = 512
STEP = 5
WIDTH = 768
FF = 3072
PAIRS = HEADS // 2
LANES = 128
OFFS = 2 * ROWS
BAND = 3 * LANES

NORM_EPS = 1e-06
BETA_ONE = 0.9
BETA_TWO = 0.999
ADAM_EPS = 1e-06
DECAY = 0.01
RATE = 0.5
FAR = 2.0**40
MIB = 1024 * 1024

F32 = jnp.float32
BF16 = jnp.bfloat16


SLIGHT = pl.CostEstimate(flops=1, bytes_accessed=1, transcendentals=0)


def mm(a, b):
    return jnp.dot(a, b, preferred_element_type=F32)


def mm_nt(a, b):
    return lax.dot_general(a, b, (((1,), (1,)), ((), ())), preferred_element_type=F32)


def mm_tn(a, b):
    return lax.dot_general(a, b, (((0,), (0,)), ((), ())), preferred_element_type=F32)


def square(ref):
    return ref[...].reshape(WIDTH, WIDTH)


def inverse_rms(values):
    return lax.rsqrt(jnp.mean(values * values, axis=-1, keepdims=True) + NORM_EPS)


def norm_back(values, gain, grad):
    inv = inverse_rms(values)
    scaled = values * inv
    weighted = grad * gain
    inner = jnp.mean(weighted * scaled, axis=-1, keepdims=True)
    return inv * (weighted - scaled * inner), jnp.sum(grad * scaled, axis=0, keepdims=True)


def project_kernel(x_ref, gain_ref, w_ref, out_ref, a1_ref):
    @pl.when(pl.program_id(0) == 0)
    def _():
        x = x_ref[...].astype(F32)
        a1_ref[...] = (x * inverse_rms(x) * gain_ref[...]).astype(BF16)

    out_ref[0] = mm(a1_ref[...], square(w_ref)).astype(BF16)


def project(x, gain, weights):
    rows = x.shape[0]
    parts, _, per, _ = weights.shape
    return pl.pallas_call(
        project_kernel,
        grid=(3,),
        in_specs=[
            pl.BlockSpec((rows, WIDTH), lambda k: (0, 0)),
            pl.BlockSpec((1, WIDTH), lambda k: (0, 0)),
            pl.BlockSpec((parts, 1, per, WIDTH), lambda k: (0, k, 0, 0)),
        ],
        out_specs=[
            pl.BlockSpec((1, rows, WIDTH), lambda k: (k, 0, 0)),
            pl.BlockSpec((rows, WIDTH), lambda k: (0, 0)),
        ],
        out_shape=[
            jax.ShapeDtypeStruct((3, rows, WIDTH), BF16),
            jax.ShapeDtypeStruct((rows, WIDTH), BF16),
        ],
        compiler_params=pltpu.CompilerParams(vmem_limit_bytes=48 * MIB),
        cost_estimate=SLIGHT,
        name="project",
    )(x, gain, weights)


def split_store(core_ref, value, keep_ref, send_ref):
    parts = keep_ref.shape[:-2]
    half = keep_ref.shape[-2]
    value = value.astype(BF16).reshape(parts + (2, half, WIDTH))
    lower = value[..., 0, :, :]
    upper = value[..., 1, :, :]
    first = core_ref[0] == 0
    keep_ref[...] = jnp.where(first, lower, upper)
    send_ref[...] = jnp.where(first, upper, lower)


def store_sets(core_ref, value, step, keep_a, send_a, keep_b, send_b):
    parts, half = keep_a.shape[:-2], keep_a.shape[-2]
    value = value.astype(BF16).reshape(parts + (2, half, WIDTH))
    lower = value[..., 0, :, :]
    upper = value[..., 1, :, :]
    first = core_ref[0] == 0
    keep = jnp.where(first, lower, upper)
    send = jnp.where(first, upper, lower)

    @pl.when(step < 2)
    def _():
        keep_a[...] = keep
        send_a[...] = send

    @pl.when(step >= 2)
    def _():
        keep_b[...] = keep
        send_b[...] = send


def set_specs(block, place_of):
    spec_a = pl.BlockSpec(block, lambda t: place_of(jnp.minimum(t, 1)))
    spec_b = pl.BlockSpec(block, lambda t: place_of(jnp.maximum(t - 2, 0)))
    return [spec_a, spec_a, spec_b, spec_b]


def weight_grads_kernel(core_ref, d_ref, dml_ref, a1_ref, o_ref, *refs):
    sets, a1t_ref = refs[-5:-1], refs[-1]
    step = pl.program_id(0)

    @pl.when(step == 0)
    def _():
        a1t_ref[...] = a1_ref[...].T

    @pl.when(step < 3)
    def _():
        store_sets(core_ref, mm(a1t_ref[...], d_ref[0]), step, *sets)

    @pl.when(step == 3)
    def _():
        store_sets(core_ref, mm_tn(o_ref[...], dml_ref[...]), step, *sets)


def weight_grads(core, dqkv, dml, a1, o, parts, after=()):
    rows = a1.shape[0]
    half = WIDTH // parts // 2
    whole = lambda shape: pl.BlockSpec(shape, lambda k: (0,) * len(shape), pipeline_mode=pl.Buffered(1))
    out = jax.ShapeDtypeStruct((parts, 2, half, WIDTH), BF16)
    return pl.pallas_call(
        weight_grads_kernel,
        grid=(4,),
        in_specs=[
            pl.BlockSpec(memory_space=pltpu.SMEM),
            pl.BlockSpec((1, rows, WIDTH), lambda k: (jnp.minimum(k, 2), 0, 0)),
            whole((rows, WIDTH)),
            whole((rows, WIDTH)),
            whole((rows, WIDTH)),
        ]
        + [pl.BlockSpec(memory_space=pl.ANY)] * len(after),
        out_specs=set_specs((parts, 1, half, WIDTH), lambda n: (0, n, 0, 0)),
        out_shape=[out] * 4,
        scratch_shapes=[pltpu.VMEM((WIDTH, rows), BF16)],
        compiler_params=pltpu.CompilerParams(vmem_limit_bytes=48 * MIB),
        cost_estimate=SLIGHT,
        name="weight_grads",
    )(core, dqkv, dml, a1, o, *after)


def input_grad_kernel(d_ref, x_ref, gain_ref, dmid_ref, w_ref, *refs):
    gin_ref, gg_ref, acc_ref = refs[-3:]
    step = pl.program_id(0)

    @pl.when(step == 0)
    def _():
        acc_ref[...] = jnp.zeros_like(acc_ref)

    acc_ref[...] += mm_nt(d_ref[0], square(w_ref))

    @pl.when(step == 2)
    def _():
        x = x_ref[...].astype(F32)
        dx, dg = norm_back(x, gain_ref[...], acc_ref[...])
        gin_ref[...] = (dmid_ref[...] + dx).astype(BF16)
        gg_ref[...] = dg


def input_grad(dqkv, x, gain, dmid, weights, after=()):
    rows = x.shape[0]
    parts, _, per, _ = weights.shape
    whole = lambda shape: pl.BlockSpec(shape, lambda k: (0,) * len(shape), pipeline_mode=pl.Buffered(1))
    return pl.pallas_call(
        input_grad_kernel,
        grid=(3,),
        in_specs=[
            pl.BlockSpec((1, rows, WIDTH), lambda k: (k, 0, 0)),
            whole((rows, WIDTH)),
            whole((1, WIDTH)),
            whole((rows, WIDTH)),
            pl.BlockSpec((parts, 1, per, WIDTH), lambda k: (0, k, 0, 0)),
        ]
        + [pl.BlockSpec(memory_space=pl.ANY)] * len(after),
        out_specs=[whole((rows, WIDTH)), whole((1, WIDTH))],
        out_shape=[
            jax.ShapeDtypeStruct((rows, WIDTH), BF16),
            jax.ShapeDtypeStruct((1, WIDTH), F32),
        ],
        scratch_shapes=[pltpu.VMEM((rows, WIDTH), F32)],
        compiler_params=pltpu.CompilerParams(vmem_limit_bytes=48 * MIB),
        cost_estimate=SLIGHT,
        name="input_grad",
    )(dqkv, x, gain, dmid, weights, *after)


def own_lanes(head):
    lane = lax.broadcasted_iota(jnp.int32, (ROWS, LANES), 1)
    return lane < HD if head == 0 else lane >= HD


def attend_kernel(off_ref, mk_ref, mq_ref, q_ref, k_ref, v_ref, o_ref, p_ref, r_ref, band_ref):
    blocks = q_ref.shape[1]
    for head in range(2):
        row = jnp.broadcast_to(off_ref[0, head : head + 1, :], (LANES, OFFS))
        band_ref[head] = pltpu.roll(row, 0, 1, stride=1, stride_axis=0)
    units = [(block, head) for block in range(blocks) for head in range(2)]
    values = [v_ref[0, block].T for block in range(blocks)]
    mixed = {}

    def score(block, head):
        own = own_lanes(head)
        keys = jnp.where(own, k_ref[0, block], mk_ref[block, head])
        return mm_nt(keys, jnp.where(own, q_ref[0, block], mq_ref[block, head]))

    def soften(block, head, scores):
        tiles = []
        for c in range(ROWS // LANES):
            lo = BAND - LANES * c
            tiles.append(scores[c * LANES : (c + 1) * LANES] + band_ref[head, :, lo : lo + ROWS])
        scores = jnp.concatenate(tiles, axis=0)
        powers = jnp.exp(scores - jnp.max(scores, axis=0, keepdims=True))
        recip = 1.0 / jnp.sum(powers, axis=0, keepdims=True)
        powers = powers.astype(BF16)
        p_ref[0, block, head] = powers
        r_ref[0, block, head : head + 1] = recip
        return powers, recip

    def mix(block, head, powers, recip):
        mixed[head] = mm(values[block][head * HD : (head + 1) * HD], powers) * recip
        if head == 1:
            o_ref[block] = jnp.concatenate([mixed[0], mixed[1]], axis=0).T.astype(BF16)

    later = score(*units[0])
    last = None
    for n, unit in enumerate(units):
        scores = later
        if n + 1 < len(units):
            later = score(*units[n + 1])
        powers, recip = soften(*unit, scores)
        if last is not None:
            mix(*last)
        last = unit + (powers, recip)
    mix(*last)


def attend(off_rows, mask_keys, mask_queries, qkv):
    blocks = qkv.shape[1]
    part = lambda n: pl.BlockSpec((1, blocks, ROWS, LANES), lambda p: (n, 0, 0, p))
    masks = pl.BlockSpec((blocks, 2, ROWS, LANES), lambda p: (0, 0, 0, 0))
    return pl.pallas_call(
        attend_kernel,
        grid=(PAIRS,),
        in_specs=[pl.BlockSpec((1, 2, OFFS), lambda p: (p, 0, 0)), masks, masks, part(0), part(1), part(2)],
        out_specs=[
            pl.BlockSpec((blocks, ROWS, LANES), lambda p: (0, 0, p)),
            pl.BlockSpec((1, blocks, 2, ROWS, ROWS), lambda p: (p, 0, 0, 0, 0)),
            pl.BlockSpec((1, blocks, 2, ROWS), lambda p: (p, 0, 0, 0)),
        ],
        out_shape=[
            jax.ShapeDtypeStruct((blocks, ROWS, WIDTH), BF16),
            jax.ShapeDtypeStruct((PAIRS, blocks, 2, ROWS, ROWS), BF16),
            jax.ShapeDtypeStruct((PAIRS, blocks, 2, ROWS), F32),
        ],
        scratch_shapes=[pltpu.VMEM((2, LANES, OFFS), F32)],
        compiler_params=pltpu.CompilerParams(vmem_limit_bytes=48 * MIB),
        cost_estimate=SLIGHT,
        name="attend",
    )(off_rows, mask_keys, mask_queries, qkv, qkv, qkv)


def attend_back_kernel(q_ref, k_ref, v_ref, do_ref, p_ref, r_ref, *refs):
    d_ref, gt_ref, band_ref = refs[-3:]
    blocks = q_ref.shape[1]
    units = [(block, head) for block in range(blocks) for head in range(2)]
    zero = jnp.zeros((ROWS, LANES), BF16)
    scaled = []
    for block in range(blocks):
        recip = [jnp.broadcast_to(r_ref[0, block, head : head + 1], (HD, ROWS)) for head in range(2)]
        recip = jnp.concatenate(recip, axis=0).T
        scaled.append((do_ref[block].astype(F32) * recip).astype(BF16))
    keys = [k_ref[0, block].T for block in range(blocks)]
    sums = {}

    def score(block, head):
        return mm_nt(jnp.where(own_lanes(head), v_ref[0, block], zero), scaled[block])

    def soften_back(block, head, dp):
        powers = p_ref[0, block, head].astype(F32)
        weighted = powers * dp
        total = jnp.sum(weighted, axis=0, keepdims=True) * r_ref[0, block, head : head + 1]
        ds = weighted - powers * total
        for tile in range(7):
            add = None
            for c in range(4):
                i = tile - 3 + c
                if 0 <= i < 4:
                    part = ds[c * LANES : (c + 1) * LANES, i * LANES : (i + 1) * LANES]
                    add = part if add is None else add + part
            here = slice(tile * LANES, (tile + 1) * LANES)
            if block == 0:
                band_ref[head, :, here] = add
            else:
                band_ref[head, :, here] += add
        return ds.astype(BF16)

    def mix(block, head, dv, ds):
        dk = mm(ds, jnp.where(own_lanes(head), q_ref[0, block], zero))
        dq = mm(keys[block][head * HD : (head + 1) * HD], ds)
        if head == 0:
            sums[0] = (dq, dk, dv)
        else:
            dq0, dk0, dv0 = sums[0]
            d_ref[0, block] = jnp.concatenate([dq0, dq], axis=0).T.astype(BF16)
            d_ref[1, block] = (dk0 + dk).astype(BF16)
            d_ref[2, block] = (dv0 + dv).astype(BF16)

    later = score(*units[0])
    last = None
    for n, unit in enumerate(units):
        dp = later
        if n + 1 < len(units):
            later = score(*units[n + 1])
        block, head = unit
        dv = mm(p_ref[0, block, head], jnp.where(own_lanes(head), scaled[block], zero))
        ds = soften_back(block, head, dp)
        if last is not None:
            mix(*last)
        last = unit + (dv, ds)
    mix(*last)

    for head in range(2):
        folded = jnp.concatenate([band_ref[head], jnp.zeros((LANES, LANES), F32)], axis=1)
        size = LANES // 2
        while size >= 8:
            folded = folded[:size] + pltpu.roll(folded[size : 2 * size], OFFS - size, 1)
            size //= 2
        row = lax.broadcasted_iota(jnp.int32, (8, OFFS), 0)
        for bit in (4, 2, 1):
            folded = jnp.where((row & bit) != 0, pltpu.roll(folded, OFFS - bit, 1), folded)
        gt_ref[0, head : head + 1, :] = jnp.sum(folded, axis=0, keepdims=True)


def attend_back(qkv, do, powers, recips, first, count, before=None, after=()):
    blocks = qkv.shape[1]
    extra = (() if before is None else (before,)) + tuple(after)
    part = lambda n: pl.BlockSpec((1, blocks, ROWS, LANES), lambda p: (n, 0, 0, p + first))
    return pl.pallas_call(
        attend_back_kernel,
        grid=(count,),
        in_specs=[
            part(0),
            part(1),
            part(2),
            pl.BlockSpec((blocks, ROWS, LANES), lambda p: (0, 0, p + first)),
            pl.BlockSpec((1, blocks, 2, ROWS, ROWS), lambda p: (p + first, 0, 0, 0, 0)),
            pl.BlockSpec((1, blocks, 2, ROWS), lambda p: (p + first, 0, 0, 0)),
        ]
        + [pl.BlockSpec(memory_space=pl.ANY)] * len(extra),
        out_specs=[
            pl.BlockSpec((3, blocks, ROWS, LANES), lambda p: (0, 0, 0, p + first)),
            pl.BlockSpec((1, 2, OFFS), lambda p: (p, 0, 0)),
        ],
        out_shape=[
            jax.ShapeDtypeStruct((3, blocks, ROWS, WIDTH), BF16),
            jax.ShapeDtypeStruct((count, 2, OFFS), F32),
        ],
        input_output_aliases={} if before is None else {6: 0},
        scratch_shapes=[pltpu.VMEM((2, LANES, 7 * LANES), F32)],
        compiler_params=pltpu.CompilerParams(vmem_limit_bytes=48 * MIB),
        cost_estimate=SLIGHT,
        name="attend_back",
    )(qkv, qkv, qkv, do, powers, recips, *extra)


def gelu_pair(u):
    c = 0.7978845608028654
    sq = u * u
    th = jnp.tanh(u * (c + (c * 0.044715) * sq))
    half = 0.5 * th + 0.5
    slope = half + (0.5 * u) * (1.0 - th * th) * (c + (3.0 * c * 0.044715) * sq)
    return u * half, slope


def feed_kernel(core_ref, x_ref, o_ref, dyl_ref, gain_ref, wo_ref, wi_ref, wf_ref,
                f_ref, mid_ref, dmid_ref, do_ref, dml_ref, wi_keep, wi_send, wf_keep, wf_send, gg_ref,
                a2_ref, a2t_ref, du_ref):
    step = pl.program_id(0)
    rows = x_ref.shape[0]
    chunk = ROWS

    @pl.when(step == 0)
    def _():
        wo = square(wo_ref)
        for at in range(0, rows, chunk):
            here = pl.ds(at, chunk)
            mid = x_ref[here].astype(F32) + mm(o_ref[here], wo)
            mid_ref[here] = mid
            a2_ref[here] = (mid * inverse_rms(mid) * gain_ref[...]).astype(BF16)
            dmid_ref[here] = jnp.zeros((chunk, WIDTH), F32)
        a2t_ref[...] = a2_ref[...].T

    wi = square(wi_ref)
    wf = square(wf_ref)
    for at in range(0, rows, chunk):
        here = pl.ds(at, chunk)
        u = mm(a2_ref[here], wi)
        da = mm_nt(dyl_ref[here], wf)
        f, slope = gelu_pair(u)
        f = f.astype(BF16)
        du = (da * slope).astype(BF16)
        f_ref[here] = f
        du_ref[here] = du
        dmid_ref[here] += mm_nt(du, wi)
    split_store(core_ref, mm_tn(f_ref[...], dyl_ref[...]), wf_keep, wf_send)
    split_store(core_ref, mm(a2t_ref[...], du_ref[...]), wi_keep, wi_send)

    @pl.when(step == pl.num_programs(0) - 1)
    def _():
        gg = jnp.zeros((1, WIDTH), F32)
        wo = square(wo_ref)
        for at in range(0, rows, chunk):
            here = pl.ds(at, chunk)
            dm, dg = norm_back(mid_ref[here], gain_ref[...], dmid_ref[here])
            gg += dg
            dm = dm + dyl_ref[here].astype(F32)
            dmid_ref[here] = dm
            low = dm.astype(BF16)
            dml_ref[here] = low
            do_ref[here] = mm_nt(low, wo).astype(BF16)
        gg_ref[...] = gg


def feed(core, x, o, dyl, gain, rest):
    rows = x.shape[0]
    parts, _, per, _ = rest.shape
    group = WIDTH // (4 * per) if parts > 1 else 1
    wf_map = (lambda t: (t, 0, 0, 0)) if parts > 1 else (lambda t: (0, t, 0, 0))
    wf_block = (group, 4, per, WIDTH) if parts > 1 else (1, 1, per, WIDTH)
    half = per // 2
    wf_half = pl.BlockSpec(wf_block[:2] + (half, WIDTH), wf_map)
    wi_half = pl.BlockSpec((parts, 1, half, WIDTH), lambda t: (0, t, 0, 0))
    halves = jax.ShapeDtypeStruct((parts, 4, half, WIDTH), BF16)
    one = (parts, 1, per, WIDTH)
    whole = lambda shape: pl.BlockSpec(shape, lambda t: (0,) * len(shape), pipeline_mode=pl.Buffered(1))
    full = (rows, WIDTH)
    return pl.pallas_call(
        feed_kernel,
        grid=(FF // WIDTH,),
        in_specs=[
            pl.BlockSpec(memory_space=pltpu.SMEM),
            whole(full),
            whole(full),
            whole(full),
            whole((1, WIDTH)),
            pl.BlockSpec(one, lambda t: (0, 8, 0, 0), pipeline_mode=pl.Buffered(1)),
            pl.BlockSpec(one, lambda t: (0, 4 + t, 0, 0)),
            pl.BlockSpec(wf_block, wf_map),
        ],
        out_specs=[
            pl.BlockSpec(full, lambda t: (0, t)),
            whole(full),
            whole(full),
            whole(full),
            whole(full),
            wi_half,
            wi_half,
            wf_half,
            wf_half,
            whole((1, WIDTH)),
        ],
        out_shape=[
            jax.ShapeDtypeStruct((rows, FF), BF16),
            jax.ShapeDtypeStruct(full, F32),
            jax.ShapeDtypeStruct(full, F32),
            jax.ShapeDtypeStruct(full, BF16),
            jax.ShapeDtypeStruct(full, BF16),
            halves,
            halves,
            halves,
            halves,
            jax.ShapeDtypeStruct((1, WIDTH), F32),
        ],
        scratch_shapes=[
            pltpu.VMEM(full, BF16),
            pltpu.VMEM((WIDTH, rows), BF16),
            pltpu.VMEM(full, BF16),
        ],
        compiler_params=pltpu.CompilerParams(vmem_limit_bytes=48 * MIB),
        cost_estimate=SLIGHT,
        name="feed",
    )(core, x, o, dyl, gain, rest, rest, rest)


def block_out_kernel(mid_ref, f_ref, wf_ref, *refs):
    out_ref, acc_ref = refs[-2:]
    step = pl.program_id(0)

    @pl.when(step == 0)
    def _():
        acc_ref[...] = mid_ref[...]

    acc_ref[...] += mm(f_ref[...], square(wf_ref))

    @pl.when(step == pl.num_programs(0) - 1)
    def _():
        out_ref[...] = acc_ref[...].astype(BF16)


def block_out(mid, f, rest, after=()):
    rows = mid.shape[0]
    parts, _, per, _ = rest.shape
    full = (rows, WIDTH)
    whole = pl.BlockSpec(full, lambda t: (0, 0), pipeline_mode=pl.Buffered(1))
    if parts > 1:
        wf_spec = pl.BlockSpec((WIDTH // (4 * per), 4, per, WIDTH), lambda t: (t, 0, 0, 0))
    else:
        wf_spec = pl.BlockSpec((1, 1, per, WIDTH), lambda t: (0, t, 0, 0))
    return pl.pallas_call(
        block_out_kernel,
        grid=(FF // WIDTH,),
        in_specs=[whole, pl.BlockSpec(full, lambda t: (0, t)), wf_spec]
        + [pl.BlockSpec(memory_space=pl.ANY)] * len(after),
        out_specs=whole,
        out_shape=jax.ShapeDtypeStruct(full, BF16),
        scratch_shapes=[pltpu.VMEM(full, F32)],
        compiler_params=pltpu.CompilerParams(vmem_limit_bytes=48 * MIB),
        cost_estimate=SLIGHT,
        name="block_out",
    )(mid, f, rest, *after)


class Links:
    def __init__(self):
        dp, fsdp = lax.axis_index("dp"), lax.axis_index("fsdp")
        self.core, self.y = dp % 2, dp // 2
        self.x, self.z = fsdp % 2, fsdp // 2

    def swap(self, value, core=0, y=0, x=0, z=0):
        dp_bits, fsdp_bits = 2 * y + core, 2 * z + x
        pairs = [
            (8 * d + f, 8 * (d ^ dp_bits) + (f ^ fsdp_bits)) for d in range(4) for f in range(8)
        ]
        return lax.ppermute(value, ("dp", "fsdp"), pairs)


def place_kernel(at_ref, *refs):
    pieces, out_ref = refs[:-1], refs[-1]
    for n, piece in enumerate(pieces):
        for slot in range(4):
            spot = 3 * (4 * n + slot)
            out_ref[at_ref[spot], at_ref[spot + 1], at_ref[spot + 2]] = piece[slot]


def place(at, pieces, parts, kinds):
    half = pieces[0].shape[1]
    out = pl.pallas_call(
        place_kernel,
        in_specs=[pl.BlockSpec(memory_space=pltpu.SMEM)]
        + [pl.BlockSpec(memory_space=pltpu.VMEM)] * len(pieces),
        out_specs=pl.BlockSpec(memory_space=pltpu.VMEM),
        out_shape=jax.ShapeDtypeStruct((parts, kinds, 2, half, WIDTH), BF16),
        compiler_params=pltpu.CompilerParams(vmem_limit_bytes=24 * MIB),
        name="place",
    )(at, *pieces)
    return out.reshape(parts, kinds, 2 * half, WIDTH)


def fetch_weights(links, shard):
    half = shard.shape[1] // 2
    mine = lax.dynamic_slice_in_dim(shard, links.core * half, half, axis=1)
    both = mine[0]
    one = lax.dynamic_index_in_dim(mine, 1 + links.y, 0, keepdims=False)
    first = jnp.stack([both, one])
    level = jnp.stack([first, links.swap(first, z=2)], axis=1)
    more = links.swap(level, z=1)
    level_a = jnp.concatenate([level[1], more[1]])
    level_b = jnp.concatenate([level[0], more[0]])
    across_a = links.swap(level_a, x=1)
    over_a = links.swap(level_a, y=1)
    across_b = links.swap(level_b, x=1)
    over_across = links.swap(across_a, y=1)
    pieces, at = [], []
    for value, kind, x_bit in (
        (level_a, 1 + links.y, 0),
        (level_b, 0, 0),
        (across_a, 1 + links.y, 1),
        (over_a, 2 - links.y, 0),
        (across_b, 0, 1),
        (over_across, 2 - links.y, 1),
    ):
        for piece, core in ((value, links.core), (links.swap(value, core=1), 1 - links.core)):
            pieces.append(piece)
            for slot in range(4):
                z = links.z ^ ((slot % 2) * 2 + slot // 2)
                at += [2 * z + (links.x ^ x_bit), kind, core]
    at = jnp.stack([jnp.asarray(v, jnp.int32) for v in at])
    return place(at, pieces, 8, 3)


def pick(value, index, axis):
    return lax.dynamic_index_in_dim(value, index, axis, keepdims=False)


def added(a, b):
    return a.astype(F32) + b.astype(F32)


def by_x(value):
    return value.reshape((4, 2) + value.shape[1:])


def lanes(value, which):
    cut = WIDTH // 2
    return lax.dynamic_slice_in_dim(value, which * cut, cut, axis=value.ndim - 1)


class GradSum:
    def __init__(self, links, keep_a, send_a, keep_b, send_b):
        self.links = links
        self.a, self.b = keep_a, keep_b
        self.sent = (send_a, send_b)
        self.got = tuple(links.swap(v, core=1) for v in self.sent)

    def wait(self, *others):
        self.got = tuple(lax.optimization_barrier(self.got + others))[: len(self.got)]

    def first(self):
        links, a, b = self.links, self.a, self.b
        got_a, got_b = self.got
        go_a = added(lanes(a, 1 - links.y), lanes(got_a, 1 - links.y)).astype(BF16)
        go_b = added(pick(by_x(b), 1 - links.x, 1), pick(by_x(got_b), 1 - links.x, 1)).astype(BF16)
        self.sent = (go_a, go_b)
        self.got = (links.swap(go_a, y=1), links.swap(go_b, x=1))
        self.a = added(lanes(a, links.y), lanes(got_a, links.y)).astype(BF16)
        self.b = added(pick(by_x(b), links.x, 1), pick(by_x(got_b), links.x, 1)).astype(BF16)

    def second(self):
        links, a, b = self.links, self.a, self.b
        got_a, got_b = self.got
        go_a = added(pick(by_x(a), 1 - links.x, 1), pick(by_x(got_a), 1 - links.x, 1)).astype(BF16)
        go_b = added(lanes(b, 1 - links.y), lanes(got_b, 1 - links.y)).astype(BF16)
        self.sent = (go_a, go_b)
        self.got = (links.swap(go_a, x=1), links.swap(go_b, y=1))
        self.a = added(pick(by_x(a), links.x, 1), pick(by_x(got_a), links.x, 1)).astype(BF16)
        self.b = added(lanes(b, links.y), lanes(got_b, links.y)).astype(BF16)

    def third(self):
        links = self.links
        got_a, got_b = self.got

        def at_z(z):
            a = added(pick(self.a, z, 0), pick(got_a, z, 0))
            b = added(pick(self.b, z, 0), pick(got_b, z, 0))
            return jnp.concatenate([a, b])

        self.sent = tuple(at_z(links.z ^ bits).astype(BF16) for bits in (2, 3, 1))
        self.got = tuple(links.swap(v, z=bits) for v, bits in zip(self.sent, (2, 3, 1)))
        self.total = at_z(links.z)

    def third_by_collective(self):
        got_a, got_b = self.got
        total = jnp.concatenate([added(self.a, got_a), added(self.b, got_b)], axis=1).astype(BF16)
        kinds, half, cut = total.shape[1:]
        self.total = total
        groups = [[2 * z + x for z in range(4)] for x in range(2)]
        self.mine = lax.psum_scatter(
            total.reshape(-1, cut), "fsdp", scatter_dimension=0, tiled=True, axis_index_groups=groups
        )

    def gather(self, *others):
        mine = tie(self.mine, *others)
        return lax.all_gather(mine, "dp", axis=0, tiled=True).reshape((4,) + self.total.shape[1:])

    def sum_up(self):
        total = self.total
        for part in self.got:
            total = total + part.astype(F32)
        self.total = total.astype(BF16)

    def last(self, *others):
        links = self.links
        total = self.total
        other = tie(links.swap(total, y=1), *others)
        left = jnp.where(links.y == 0, total, other)
        right = jnp.where(links.y == 0, other, total)
        mine = jnp.concatenate([left, right], axis=-1)
        return mine, links.swap(mine, core=1)


def tie(value, *others):
    return lax.optimization_barrier((value,) + others)[0]


def sum_small(links, value, steps, marks=()):
    for n, step in enumerate(steps):
        if n < len(marks):
            value = tie(value, *marks[n])
        value = value + links.swap(value, **step)
    return value


FSDP_STEPS = (dict(z=2), dict(z=1), dict(x=1))
ALL_STEPS = (dict(core=1), dict(x=1), dict(y=1), dict(z=2), dict(z=1))


def moments(weight, first, second, grad):
    first_new = BETA_ONE * first + (1.0 - BETA_ONE) * grad
    second_new = BETA_TWO * second + (1.0 - BETA_TWO) * grad * grad
    root = jnp.sqrt(second_new * (1.0 / (1.0 - BETA_TWO**STEP)))
    direction = first_new * (1.0 / (1.0 - BETA_ONE**STEP)) / (root + ADAM_EPS) + DECAY * weight
    return (first_new, second_new, direction)


def update_piece(weight_ref, first_ref, second_ref, grads, m_out, v_out, r_out):
    half = grads[0].shape[0]
    squares = [jnp.zeros((1, WIDTH), F32)] * 2
    for part in range(2):
        here = pl.ds(part * half, half)
        weight = weight_ref[here]
        m_new, v_new, r = moments(weight, first_ref[here], second_ref[here], grads[part])
        m_out[here] = m_new
        v_out[here] = v_new
        r_out[here] = r
        squares[0] += jnp.sum(weight * weight, axis=0, keepdims=True)
        squares[1] += jnp.sum(r * r, axis=0, keepdims=True)
    return jnp.concatenate(squares, axis=0)


def update_attn_kernel(core_ref, other_ref, mine_ref, theirs_ref, p_ref, m_ref, v_ref,
                       m_out, v_out, last_out, r_out, sum_out):
    first = core_ref[0] == 0
    sums = other_ref[...]
    lane = lax.broadcasted_iota(jnp.int32, sums.shape, 1)
    for n in range(4):
        mine, theirs = mine_ref[n].astype(F32), theirs_ref[n].astype(F32)
        grads = (jnp.where(first, mine, theirs), jnp.where(first, theirs, mine))
        second_out = v_out.at[n] if n < 3 else last_out
        squares = update_piece(
            p_ref.at[n], m_ref.at[n], v_ref.at[n], grads, m_out.at[n], second_out, r_out.at[n]
        )
        sums = jnp.where(lane == n, jnp.sum(squares, axis=1, keepdims=True), sums)
    sum_out[...] = sums


def update_attn(core, other, mine, theirs, arrays):
    like = jax.ShapeDtypeStruct(arrays[0].shape, F32)
    per = like.shape[1]
    whole = lambda shape: pl.BlockSpec(shape, lambda k: (0,) * len(shape))
    shapes = [like.shape, (3, per, WIDTH), (per, WIDTH), like.shape, other.shape]
    return pl.pallas_call(
        update_attn_kernel,
        grid=(1,),
        in_specs=[pl.BlockSpec(memory_space=pltpu.SMEM), whole(other.shape)]
        + [whole(mine.shape)] * 2
        + [whole(like.shape)] * 3,
        out_specs=[whole(shape) for shape in shapes],
        out_shape=[jax.ShapeDtypeStruct(shape, F32) for shape in shapes],
        compiler_params=pltpu.CompilerParams(vmem_limit_bytes=60 * MIB),
        cost_estimate=SLIGHT,
        name="update_attn",
    )(core, other, mine, theirs, *arrays)


def update_feed_kernel(out_grad, in_grad, *refs):
    arrays, (sum_out,) = refs[:12], refs[12:]
    for n, grad in enumerate((out_grad, in_grad)):
        pieces = [grad[place, 0].astype(F32) for place in range(4)]
        grads = [jnp.concatenate([pieces[part], pieces[2 + part]], axis=1) for part in range(2)]
        ins, outs = arrays[3 * n : 3 * n + 3], arrays[6 + 3 * n : 9 + 3 * n]
        sum_out[0, n] = update_piece(*ins, grads, *outs)


def update_feed(grads, out_arrays, in_arrays):
    per = in_arrays[0].shape[0]
    quarter = (4, 1) + grads.shape[2:]
    out_block = pl.BlockSpec((per, WIDTH), lambda k: (k, 0))
    in_block = pl.BlockSpec((per, WIDTH), lambda k: (0, k))
    blocks = [out_block] * 3 + [in_block] * 3
    return pl.pallas_call(
        update_feed_kernel,
        grid=(4,),
        in_specs=[
            pl.BlockSpec(quarter, lambda k: (0, k, 0, 0)),
            pl.BlockSpec(quarter, lambda k: (0, k + 4, 0, 0)),
        ]
        + blocks,
        out_specs=blocks + [pl.BlockSpec((1, 2, 2, WIDTH), lambda k: (k, 0, 0, 0))],
        out_shape=[jax.ShapeDtypeStruct(v.shape, F32) for v in out_arrays + in_arrays]
        + [jax.ShapeDtypeStruct((4, 2, 2, WIDTH), F32)],
        compiler_params=pltpu.CompilerParams(vmem_limit_bytes=60 * MIB),
        cost_estimate=SLIGHT,
        name="update_feed",
    )(grads, grads, *out_arrays, *in_arrays)


def apply_kernel(sums_ref, gains_p, gains_r, table_p, table_r, attn_w, attn_r, in_w, in_r, out_w, out_r,
                 attn_ref, in_ref, out_ref, gains_ref, table_ref, norms_ref):
    step = pl.program_id(0)
    norms = jnp.sqrt(sums_ref[...])
    scale = RATE * (norms[0:1] / (norms[1:2] + ADAM_EPS))
    lane = lax.broadcasted_iota(jnp.int32, scale.shape, 1)
    take = lambda n: jnp.sum(jnp.where(lane == n, scale, 0.0), axis=1, keepdims=True)
    attn_ref[0] = attn_w[0] - take(step) * attn_r[0]
    in_ref[...] = in_w[...] - take(4) * in_r[...]
    out_ref[...] = out_w[...] - take(5) * out_r[...]

    @pl.when(step == 0)
    def _():
        for n in range(2):
            gains_ref[n : n + 1] = gains_p[n : n + 1] - take(6 + n) * gains_r[n : n + 1]
        table_ref[...] = table_p[...] - take(8) * table_r[...]
        square_of = (norms_ref.shape[0], scale.shape[1])
        here = lax.broadcasted_iota(jnp.int32, square_of, 0) == lax.broadcasted_iota(jnp.int32, square_of, 1)
        for n in range(2):
            column = jnp.where(here, jnp.broadcast_to(norms[n : n + 1], square_of), 0.0)
            norms_ref[:, n : n + 1] = jnp.sum(column, axis=1, keepdims=True)


def apply(sums, gains, table, attn, ffin, ffout):
    per = ffin[0].shape[0]
    whole = lambda v: pl.BlockSpec(v.shape, lambda k: (0,) * len(v.shape))
    specs = [
        pl.BlockSpec((1, per, WIDTH), lambda k: (k, 0, 0)),
        pl.BlockSpec((per, WIDTH), lambda k: (0, k)),
        pl.BlockSpec((per, WIDTH), lambda k: (k, 0)),
    ]
    norms = jax.ShapeDtypeStruct((9, 2), F32)
    return pl.pallas_call(
        apply_kernel,
        grid=(4,),
        in_specs=[whole(v) for v in (sums, *gains, *table)] + [spec for spec in specs for _ in range(2)],
        out_specs=specs + [whole(gains[0]), whole(table[0]), whole(norms)],
        out_shape=[jax.ShapeDtypeStruct(v[0].shape, F32) for v in (attn, ffin, ffout, gains, table)] + [norms],
        compiler_params=pltpu.CompilerParams(vmem_limit_bytes=60 * MIB),
        cost_estimate=SLIGHT,
        name="apply",
    )(sums, *gains, *table, *attn, *ffin, *ffout)


def row_labels(lengths):
    ends = jnp.cumsum(lengths, axis=1)
    places = jnp.arange(ROWS, dtype=jnp.int32)
    labels = jnp.sum((places[None, :, None] >= ends[:, None, :]).astype(jnp.int32), axis=2)
    return labels, places[None, :] < ends[:, -1:]


def label_masks(labels, count):
    codes = jnp.arange(HD)
    equal = labels[:, :, None] == codes
    keys = jnp.where(equal | (codes >= count), 0.0, 1.0).astype(BF16)
    queries = jnp.where(equal, -FAR, 0.0).astype(BF16)
    none = jnp.zeros_like(keys)
    sides = lambda v: jnp.stack(
        [jnp.concatenate([none, v], axis=-1), jnp.concatenate([v, none], axis=-1)], axis=1
    )
    return sides(keys), sides(queries)


def body(
    tokens, cotangent, seg_lengths, bucket_of,
    attn_w, attn_m, attn_v, ffin_w, ffin_m, ffin_v, ffout_w, ffout_m, ffout_v,
    gains, gains_m, gains_v, table, table_m, table_v,
):
    fsdp = lax.axis_size("fsdp")
    dp = lax.axis_size("dp")
    both = ("fsdp", "dp")
    batches, count, width = tokens.shape
    rows = batches * count
    blocks = rows // ROWS
    per = attn_w.shape[1]
    direct = per % 32 == 0
    paired = direct and fsdp == 8 and dp == 4
    links = Links() if paired else None
    core = (links.core if paired else jnp.int32(0)).reshape(1)

    me = lax.axis_index("dp")

    def spread(shard):
        flat = shard.reshape(-1, WIDTH)
        size = flat.shape[0] // dp
        mine = lax.dynamic_slice_in_dim(flat, me * size, size, axis=0)
        return lax.all_gather(mine, both, axis=0, tiled=True).reshape((fsdp,) + shard.shape)

    def whole_of(gathered):
        kinds = gathered.shape[1]
        return gathered.transpose(1, 0, 2, 3).reshape(1, kinds, WIDTH, WIDTH)

    attn_low = attn_w.astype(BF16)
    ffin_low = ffin_w.astype(BF16).reshape(per, 4, WIDTH).transpose(1, 0, 2)
    ffout_low = ffout_w.astype(BF16).reshape(4, per, WIDTH)
    qkv_w = fetch_weights(links, attn_low[:3]) if paired else spread(attn_low[:3])
    rest_w = spread(jnp.concatenate([ffout_low, ffin_low, attn_low[3:]], axis=0))
    if not direct:
        qkv_w = whole_of(qkv_w)
        wf_all = rest_w[:, :4].reshape(1, 4, WIDTH, WIDTH)
        rest_w = jnp.concatenate([wf_all, whole_of(rest_w[:, 4:])], axis=1)
    small = jnp.concatenate([gains.reshape(-1), table.reshape(-1)]).astype(BF16)
    if paired:
        own = jnp.arange(fsdp)[:, None] == lax.axis_index("fsdp")
        small = sum_small(links, jnp.where(own, small[None].astype(F32), 0.0), FSDP_STEPS).astype(BF16)
    else:
        small = lax.all_gather(small, "fsdp", axis=0)
    gain_full = small[:, : 2 * per].reshape(fsdp, 2, per).transpose(1, 0, 2).reshape(2, 1, width).astype(F32)
    table_full = small[:, 2 * per :].reshape(BUCKETS, HEADS)

    padded = jnp.concatenate([bucket_of, jnp.full((1,), -1, jnp.int32)])
    padded = jnp.roll(padded[::-1], -(OFFS - 1 - 7 * LANES + 1))
    onehot = (padded[None, :] == jnp.arange(BUCKETS, dtype=jnp.int32)[:, None]).astype(BF16)
    off_rows = lax.dot_general(
        table_full, onehot, (((0,), (0,)), ((), ())), preferred_element_type=F32
    ).reshape(PAIRS, 2, OFFS)

    labels, valid = row_labels(seg_lengths.reshape(blocks, -1))
    mask_keys, mask_queries = label_masks(labels, seg_lengths.shape[-1] + 1)
    x = tokens.reshape(rows, width)
    dyl = jnp.where(valid.reshape(rows, 1), cotangent.reshape(rows, width), jnp.zeros((), BF16))

    qkv, a1 = project(x, gain_full[0], qkv_w)
    qkv = qkv.reshape(3, blocks, ROWS, width)
    o, powers, recips = attend(off_rows, mask_keys, mask_queries, qkv)
    f, mid, dmid, do, dml, wi_keep, wi_send, wf_keep, wf_send, gg2 = feed(
        core, x, o.reshape(rows, width), dyl, gain_full[1], rest_w
    )
    do = do.reshape(blocks, ROWS, width)
    o = o.reshape(rows, width)
    parts = qkv_w.shape[0]
    if paired:
        feed_sum = GradSum(links, wf_keep, wf_send, wi_keep, wi_send)
        dqkv, gt0 = attend_back(qkv, do, powers, recips, 0, 2)
        feed_sum.wait(gt0)
        feed_sum.first()
        dqkv, gt1 = attend_back(qkv, do, powers, recips, 2, 2, dqkv, feed_sum.sent)
        dqkv, gt2 = attend_back(qkv, do, powers, recips, 4, 2, dqkv)
        dqkv = dqkv.reshape(3, rows, width)
        out = block_out(mid, f, rest_w, (gt2,))
        feed_sum.wait(out)
        feed_sum.second()
        attn_sets = list(weight_grads(core, dqkv, dml, a1, o, parts, feed_sum.sent))
        feed_sum.wait(attn_sets[0])
        feed_sum.third_by_collective()
        attn_sets[1], attn_sets[3] = (tie(attn_sets[n], feed_sum.total) for n in (1, 3))
        attn_sum = GradSum(links, *attn_sets)
        attn_sum.first()
        gin, gg1 = input_grad(dqkv, x, gain_full[0], dmid, qkv_w, attn_sum.sent)
        attn_sum.wait(gg1)
        attn_sum.second()
        marks = [attn_sum.sent]
        attn_sum.third()
        marks += [attn_sum.sent] * 2
        feed_grads = feed_sum.gather(*attn_sum.sent)
        attn_sum.sum_up()
        feed_grads = tie(feed_grads, attn_sum.total)
        gt = jnp.concatenate([gt0, gt1, gt2])
    else:
        dqkv, gt = attend_back(qkv, do, powers, recips, 0, PAIRS)
        dqkv = dqkv.reshape(3, rows, width)
        out = block_out(mid, f, rest_w)
        attn_sets = weight_grads(core, dqkv, dml, a1, o, parts)
        gin, gg1 = input_grad(dqkv, x, gain_full[0], dmid, qkv_w)
    grad_table = lax.dot_general(
        onehot.astype(F32), gt.reshape(HEADS, OFFS), (((1,), (1,)), ((), ())),
        preferred_element_type=F32, precision=lax.Precision.HIGHEST,
    )

    def parts_of(grad):
        kinds = grad.shape[1]
        return grad.reshape(kinds, fsdp, per, WIDTH).transpose(1, 0, 2, 3)

    def gather_sum(grad):
        kinds = grad.shape[1]
        flat = grad.reshape(fsdp * kinds * per, WIDTH)
        mine = lax.psum_scatter(flat, both, scatter_dimension=0, tiled=True)
        return lax.all_gather(mine, "dp", axis=0, tiled=True).reshape(kinds, per, WIDTH).astype(F32)

    if not paired:
        dwf = jnp.concatenate([wf_keep, wf_send], axis=2).reshape(fsdp, 4, per, WIDTH)
        dwi = jnp.concatenate([wi_keep, wi_send], axis=2)
        dw = [jnp.concatenate(attn_sets[n : n + 2], axis=2) for n in (0, 2)]
        dw = jnp.concatenate(dw, axis=1)
        if not direct:
            dwi, dw = parts_of(dwi), parts_of(dw)
        half, cut = per // 2, WIDTH // 2
        feed_grads = gather_sum(jnp.concatenate([dwf, dwi], axis=1)).reshape(8, 2, half, 2, cut)
        feed_grads = feed_grads.transpose(3, 1, 0, 2, 4).reshape(4, 8, half, cut)
        attn_grads = gather_sum(dw)
        attn_mine, attn_theirs = attn_grads[:, :half], attn_grads[:, half:]
        marks = []

    grad_gains = jnp.concatenate([gg1, gg2], axis=0).reshape(2, fsdp, per).transpose(1, 0, 2).reshape(fsdp, -1)
    grad_small = jnp.concatenate([grad_gains, grad_table.reshape(fsdp, -1)], axis=1)
    out_m, out_v, out_r, in_m, in_v, in_r, feed_sq = update_feed(
        feed_grads, (ffout_w, ffout_m, ffout_v), (ffin_w, ffin_m, ffin_v)
    )
    if paired:
        attn_mine, attn_theirs = attn_sum.last(feed_sq)
    feed_sq = jnp.sum(feed_sq, axis=(0, 3))[::-1].T
    if paired:
        marks += [(attn_sum.total,)]
        grad_small = sum_small(links, grad_small, ALL_STEPS, marks)
    else:
        grad_small = lax.psum(grad_small, ("dp", "fsdp"))
    grad_small = lax.dynamic_index_in_dim(grad_small, lax.axis_index("fsdp"), 0, keepdims=False)

    flat = lambda a, b: jnp.concatenate([a.reshape(-1), b.reshape(-1)])
    small_p = flat(gains, table)
    small_m, small_v, small_r = moments(small_p, flat(gains_m, table_m), flat(gains_v, table_v), grad_small)
    kind = jnp.minimum(jnp.arange(small_p.shape[0]) // per, 2)
    member = kind[None, :] == jnp.arange(3)[:, None]
    squares = lambda v: jnp.sum(jnp.where(member, (v * v)[None], 0.0), axis=1)

    def unpack(v):
        return v[: 2 * per].reshape(2, per), v[2 * per :].reshape(table.shape)

    gains_r, table_r = unpack(small_r)
    gains_m_new, table_m_new = unpack(small_m)
    gains_v_new, table_v_new = unpack(small_v)

    other = jnp.concatenate([feed_sq, jnp.stack([squares(small_p), squares(small_r)])], axis=1)
    other = jnp.pad(other, ((0, 0), (4, LANES - 9)))
    attn_new_m, attn_new_v, out_new_v, attn_r, sums = update_attn(
        core, other, attn_mine, attn_theirs, (attn_w, attn_m, attn_v)
    )
    sums = sum_small(links, sums, FSDP_STEPS) if paired else lax.psum(sums, "fsdp")
    attn_new, ffin_new, ffout_new, gains_new, table_new, norms = apply(
        sums, (gains, gains_r), (table, table_r), (attn_w, attn_r), (ffin_w, in_r), (ffout_w, out_r)
    )
    return (
        out.reshape(tokens.shape),
        gin.reshape(tokens.shape),
        attn_new, attn_new_m, attn_new_v, out_new_v,
        ffin_new, in_m, in_v,
        ffout_new, out_m, out_v,
        gains_new, gains_m_new, gains_v_new,
        table_new, table_m_new, table_v_new,
        norms,
    )


def solution(mesh):
    batch = P(None, ("dp", "fsdp"), None)
    mid_dim = P(None, "fsdp", None)
    first = P("fsdp", None)
    last = P(None, "fsdp")
    in_specs = (batch, batch, batch, P()) + (mid_dim,) * 3 + (first,) * 6 + (last,) * 3 + (first,) * 3
    out_specs = (batch, batch) + (mid_dim,) * 3 + (first,) * 7 + (last,) * 3 + (first,) * 3 + (P(),)
    return jax.shard_map(body, mesh=mesh, in_specs=in_specs, out_specs=out_specs, check_vma=False)
```

```python
import jax
import jax.numpy as jnp
from jax import lax
from jax.experimental import pallas as pl
from jax.experimental.pallas import tpu as pltpu
from jax.sharding import PartitionSpec as P

HEADS = 12
HD = 64
BUCKETS = 32
ROWS = 512
STEP = 5
WIDTH = 768
FF = 3072
PAIRS = HEADS // 2
LANES = 128
OFFS = 2 * ROWS
BAND = 3 * LANES

NORM_EPS = 1e-06
BETA_ONE = 0.9
BETA_TWO = 0.999
ADAM_EPS = 1e-06
DECAY = 0.01
RATE = 0.5
FAR = 2.0**40
MIB = 1024 * 1024

F32 = jnp.float32
BF16 = jnp.bfloat16


SLIGHT = pl.CostEstimate(flops=1, bytes_accessed=1, transcendentals=0)


def mm(a, b):
    return jnp.dot(a, b, preferred_element_type=F32)


def mm_nt(a, b):
    return lax.dot_general(a, b, (((1,), (1,)), ((), ())), preferred_element_type=F32)


def mm_tn(a, b):
    return lax.dot_general(a, b, (((0,), (0,)), ((), ())), preferred_element_type=F32)


def square(ref):
    return ref[...].reshape(WIDTH, WIDTH)


def inverse_rms(values):
    return lax.rsqrt(jnp.mean(values * values, axis=-1, keepdims=True) + NORM_EPS)


def norm_back(values, gain, grad):
    inv = inverse_rms(values)
    scaled = values * inv
    weighted = grad * gain
    inner = jnp.mean(weighted * scaled, axis=-1, keepdims=True)
    return inv * (weighted - scaled * inner), jnp.sum(grad * scaled, axis=0, keepdims=True)


def project_kernel(x_ref, gain_ref, w_ref, out_ref, a1_ref):
    @pl.when(pl.program_id(0) == 0)
    def _():
        x = x_ref[...].astype(F32)
        a1_ref[...] = (x * inverse_rms(x) * gain_ref[...]).astype(BF16)

    out_ref[0] = mm(a1_ref[...], square(w_ref)).astype(BF16)


def project(x, gain, weights):
    rows = x.shape[0]
    parts, _, per, _ = weights.shape
    return pl.pallas_call(
        project_kernel,
        grid=(3,),
        in_specs=[
            pl.BlockSpec((rows, WIDTH), lambda k: (0, 0)),
            pl.BlockSpec((1, WIDTH), lambda k: (0, 0)),
            pl.BlockSpec((parts, 1, per, WIDTH), lambda k: (0, k, 0, 0)),
        ],
        out_specs=[
            pl.BlockSpec((1, rows, WIDTH), lambda k: (k, 0, 0)),
            pl.BlockSpec((rows, WIDTH), lambda k: (0, 0)),
        ],
        out_shape=[
            jax.ShapeDtypeStruct((3, rows, WIDTH), BF16),
            jax.ShapeDtypeStruct((rows, WIDTH), BF16),
        ],
        compiler_params=pltpu.CompilerParams(vmem_limit_bytes=48 * MIB),
        cost_estimate=SLIGHT,
        name="project",
    )(x, gain, weights)


def split_store(core_ref, value, keep_ref, send_ref):
    parts = keep_ref.shape[:-2]
    half = keep_ref.shape[-2]
    value = value.astype(BF16).reshape(parts + (2, half, WIDTH))
    lower = value[..., 0, :, :]
    upper = value[..., 1, :, :]
    first = core_ref[0] == 0
    keep_ref[...] = jnp.where(first, lower, upper)
    send_ref[...] = jnp.where(first, upper, lower)


def store_sets(core_ref, value, step, keep_a, send_a, keep_b, send_b):
    parts, half = keep_a.shape[:-2], keep_a.shape[-2]
    value = value.astype(BF16).reshape(parts + (2, half, WIDTH))
    lower = value[..., 0, :, :]
    upper = value[..., 1, :, :]
    first = core_ref[0] == 0
    keep = jnp.where(first, lower, upper)
    send = jnp.where(first, upper, lower)

    @pl.when(step < 2)
    def _():
        keep_a[...] = keep
        send_a[...] = send

    @pl.when(step >= 2)
    def _():
        keep_b[...] = keep
        send_b[...] = send


def set_specs(block, place_of):
    spec_a = pl.BlockSpec(block, lambda t: place_of(jnp.minimum(t, 1)))
    spec_b = pl.BlockSpec(block, lambda t: place_of(jnp.maximum(t - 2, 0)))
    return [spec_a, spec_a, spec_b, spec_b]


def weight_grads_kernel(core_ref, d_ref, dml_ref, a1_ref, o_ref, *refs):
    sets, a1t_ref = refs[-5:-1], refs[-1]
    step = pl.program_id(0)

    @pl.when(step == 0)
    def _():
        a1t_ref[...] = a1_ref[...].T

    @pl.when(step < 3)
    def _():
        store_sets(core_ref, mm(a1t_ref[...], d_ref[0]), step, *sets)

    @pl.when(step == 3)
    def _():
        store_sets(core_ref, mm_tn(o_ref[...], dml_ref[...]), step, *sets)


def weight_grads(core, dqkv, dml, a1, o, parts, after=()):
    rows = a1.shape[0]
    half = WIDTH // parts // 2
    whole = lambda shape: pl.BlockSpec(shape, lambda k: (0,) * len(shape), pipeline_mode=pl.Buffered(1))
    out = jax.ShapeDtypeStruct((parts, 2, half, WIDTH), BF16)
    return pl.pallas_call(
        weight_grads_kernel,
        grid=(4,),
        in_specs=[
            pl.BlockSpec(memory_space=pltpu.SMEM),
            pl.BlockSpec((1, rows, WIDTH), lambda k: (jnp.minimum(k, 2), 0, 0)),
            whole((rows, WIDTH)),
            whole((rows, WIDTH)),
            whole((rows, WIDTH)),
        ]
        + [pl.BlockSpec(memory_space=pl.ANY)] * len(after),
        out_specs=set_specs((parts, 1, half, WIDTH), lambda n: (0, n, 0, 0)),
        out_shape=[out] * 4,
        scratch_shapes=[pltpu.VMEM((WIDTH, rows), BF16)],
        compiler_params=pltpu.CompilerParams(vmem_limit_bytes=48 * MIB),
        cost_estimate=SLIGHT,
        name="weight_grads",
    )(core, dqkv, dml, a1, o, *after)


def input_grad_kernel(d_ref, x_ref, gain_ref, dmid_ref, w_ref, *refs):
    gin_ref, gg_ref, acc_ref = refs[-3:]
    step = pl.program_id(0)

    @pl.when(step == 0)
    def _():
        acc_ref[...] = jnp.zeros_like(acc_ref)

    acc_ref[...] += mm_nt(d_ref[0], square(w_ref))

    @pl.when(step == 2)
    def _():
        x = x_ref[...].astype(F32)
        dx, dg = norm_back(x, gain_ref[...], acc_ref[...])
        gin_ref[...] = (dmid_ref[...] + dx).astype(BF16)
        gg_ref[...] = dg


def input_grad(dqkv, x, gain, dmid, weights, after=()):
    rows = x.shape[0]
    parts, _, per, _ = weights.shape
    whole = lambda shape: pl.BlockSpec(shape, lambda k: (0,) * len(shape), pipeline_mode=pl.Buffered(1))
    return pl.pallas_call(
        input_grad_kernel,
        grid=(3,),
        in_specs=[
            pl.BlockSpec((1, rows, WIDTH), lambda k: (k, 0, 0)),
            whole((rows, WIDTH)),
            whole((1, WIDTH)),
            whole((rows, WIDTH)),
            pl.BlockSpec((parts, 1, per, WIDTH), lambda k: (0, k, 0, 0)),
        ]
        + [pl.BlockSpec(memory_space=pl.ANY)] * len(after),
        out_specs=[whole((rows, WIDTH)), whole((1, WIDTH))],
        out_shape=[
            jax.ShapeDtypeStruct((rows, WIDTH), BF16),
            jax.ShapeDtypeStruct((1, WIDTH), F32),
        ],
        scratch_shapes=[pltpu.VMEM((rows, WIDTH), F32)],
        compiler_params=pltpu.CompilerParams(vmem_limit_bytes=48 * MIB),
        cost_estimate=SLIGHT,
        name="input_grad",
    )(dqkv, x, gain, dmid, weights, *after)


def own_lanes(head):
    lane = lax.broadcasted_iota(jnp.int32, (ROWS, LANES), 1)
    return lane < HD if head == 0 else lane >= HD


def attend_kernel(off_ref, mk_ref, mq_ref, q_ref, k_ref, v_ref, o_ref, p_ref, r_ref, band_ref):
    blocks = q_ref.shape[1]
    for head in range(2):
        row = jnp.broadcast_to(off_ref[0, head : head + 1, :], (LANES, OFFS))
        band_ref[head] = pltpu.roll(row, 0, 1, stride=1, stride_axis=0)
    units = [(block, head) for block in range(blocks) for head in range(2)]
    values = [v_ref[0, block].T for block in range(blocks)]
    mixed = {}

    def score(block, head):
        own = own_lanes(head)
        keys = jnp.where(own, k_ref[0, block], mk_ref[block, head])
        return mm_nt(keys, jnp.where(own, q_ref[0, block], mq_ref[block, head]))

    def soften(block, head, scores):
        tiles = []
        for c in range(ROWS // LANES):
            lo = BAND - LANES * c
            tiles.append(scores[c * LANES : (c + 1) * LANES] + band_ref[head, :, lo : lo + ROWS])
        scores = jnp.concatenate(tiles, axis=0)
        powers = jnp.exp(scores - jnp.max(scores, axis=0, keepdims=True))
        recip = 1.0 / jnp.sum(powers, axis=0, keepdims=True)
        powers = powers.astype(BF16)
        p_ref[0, block, head] = powers
        r_ref[0, block, head : head + 1] = recip
        return powers, recip

    def mix(block, head, powers, recip):
        mixed[head] = mm(values[block][head * HD : (head + 1) * HD], powers) * recip
        if head == 1:
            o_ref[block] = jnp.concatenate([mixed[0], mixed[1]], axis=0).T.astype(BF16)

    later = score(*units[0])
    last = None
    for n, unit in enumerate(units):
        scores = later
        if n + 1 < len(units):
            later = score(*units[n + 1])
        powers, recip = soften(*unit, scores)
        if last is not None:
            mix(*last)
        last = unit + (powers, recip)
    mix(*last)


def attend(off_rows, mask_keys, mask_queries, qkv):
    blocks = qkv.shape[1]
    part = lambda n: pl.BlockSpec((1, blocks, ROWS, LANES), lambda p: (n, 0, 0, p))
    masks = pl.BlockSpec((blocks, 2, ROWS, LANES), lambda p: (0, 0, 0, 0))
    return pl.pallas_call(
        attend_kernel,
        grid=(PAIRS,),
        in_specs=[pl.BlockSpec((1, 2, OFFS), lambda p: (p, 0, 0)), masks, masks, part(0), part(1), part(2)],
        out_specs=[
            pl.BlockSpec((blocks, ROWS, LANES), lambda p: (0, 0, p)),
            pl.BlockSpec((1, blocks, 2, ROWS, ROWS), lambda p: (p, 0, 0, 0, 0)),
            pl.BlockSpec((1, blocks, 2, ROWS), lambda p: (p, 0, 0, 0)),
        ],
        out_shape=[
            jax.ShapeDtypeStruct((blocks, ROWS, WIDTH), BF16),
            jax.ShapeDtypeStruct((PAIRS, blocks, 2, ROWS, ROWS), BF16),
            jax.ShapeDtypeStruct((PAIRS, blocks, 2, ROWS), F32),
        ],
        scratch_shapes=[pltpu.VMEM((2, LANES, OFFS), F32)],
        compiler_params=pltpu.CompilerParams(vmem_limit_bytes=48 * MIB),
        cost_estimate=SLIGHT,
        name="attend",
    )(off_rows, mask_keys, mask_queries, qkv, qkv, qkv)


def attend_back_kernel(q_ref, k_ref, v_ref, do_ref, p_ref, r_ref, *refs):
    d_ref, gt_ref, band_ref = refs[-3:]
    blocks = q_ref.shape[1]
    units = [(block, head) for block in range(blocks) for head in range(2)]
    zero = jnp.zeros((ROWS, LANES), BF16)
    scaled = []
    for block in range(blocks):
        recip = [jnp.broadcast_to(r_ref[0, block, head : head + 1], (HD, ROWS)) for head in range(2)]
        recip = jnp.concatenate(recip, axis=0).T
        scaled.append((do_ref[block].astype(F32) * recip).astype(BF16))
    keys = [k_ref[0, block].T for block in range(blocks)]
    sums = {}

    def score(block, head):
        return mm_nt(jnp.where(own_lanes(head), v_ref[0, block], zero), scaled[block])

    def soften_back(block, head, dp):
        powers = p_ref[0, block, head].astype(F32)
        weighted = powers * dp
        total = jnp.sum(weighted, axis=0, keepdims=True) * r_ref[0, block, head : head + 1]
        ds = weighted - powers * total
        for tile in range(7):
            add = None
            for c in range(4):
                i = tile - 3 + c
                if 0 <= i < 4:
                    part = ds[c * LANES : (c + 1) * LANES, i * LANES : (i + 1) * LANES]
                    add = part if add is None else add + part
            here = slice(tile * LANES, (tile + 1) * LANES)
            if block == 0:
                band_ref[head, :, here] = add
            else:
                band_ref[head, :, here] += add
        return ds.astype(BF16)

    def mix(block, head, dv, ds):
        dk = mm(ds, jnp.where(own_lanes(head), q_ref[0, block], zero))
        dq = mm(keys[block][head * HD : (head + 1) * HD], ds)
        if head == 0:
            sums[0] = (dq, dk, dv)
        else:
            dq0, dk0, dv0 = sums[0]
            d_ref[0, block] = jnp.concatenate([dq0, dq], axis=0).T.astype(BF16)
            d_ref[1, block] = (dk0 + dk).astype(BF16)
            d_ref[2, block] = (dv0 + dv).astype(BF16)

    later = score(*units[0])
    last = None
    for n, unit in enumerate(units):
        dp = later
        if n + 1 < len(units):
            later = score(*units[n + 1])
        block, head = unit
        dv = mm(p_ref[0, block, head], jnp.where(own_lanes(head), scaled[block], zero))
        ds = soften_back(block, head, dp)
        if last is not None:
            mix(*last)
        last = unit + (dv, ds)
    mix(*last)

    for head in range(2):
        folded = jnp.concatenate([band_ref[head], jnp.zeros((LANES, LANES), F32)], axis=1)
        size = LANES // 2
        while size >= 8:
            folded = folded[:size] + pltpu.roll(folded[size : 2 * size], OFFS - size, 1)
            size //= 2
        row = lax.broadcasted_iota(jnp.int32, (8, OFFS), 0)
        for bit in (4, 2, 1):
            folded = jnp.where((row & bit) != 0, pltpu.roll(folded, OFFS - bit, 1), folded)
        gt_ref[0, head : head + 1, :] = jnp.sum(folded, axis=0, keepdims=True)


def attend_back(qkv, do, powers, recips, first, count, before=None, after=()):
    blocks = qkv.shape[1]
    extra = (() if before is None else (before,)) + tuple(after)
    part = lambda n: pl.BlockSpec((1, blocks, ROWS, LANES), lambda p: (n, 0, 0, p + first))
    return pl.pallas_call(
        attend_back_kernel,
        grid=(count,),
        in_specs=[
            part(0),
            part(1),
            part(2),
            pl.BlockSpec((blocks, ROWS, LANES), lambda p: (0, 0, p + first)),
            pl.BlockSpec((1, blocks, 2, ROWS, ROWS), lambda p: (p + first, 0, 0, 0, 0)),
            pl.BlockSpec((1, blocks, 2, ROWS), lambda p: (p + first, 0, 0, 0)),
        ]
        + [pl.BlockSpec(memory_space=pl.ANY)] * len(extra),
        out_specs=[
            pl.BlockSpec((3, blocks, ROWS, LANES), lambda p: (0, 0, 0, p + first)),
            pl.BlockSpec((1, 2, OFFS), lambda p: (p, 0, 0)),
        ],
        out_shape=[
            jax.ShapeDtypeStruct((3, blocks, ROWS, WIDTH), BF16),
            jax.ShapeDtypeStruct((count, 2, OFFS), F32),
        ],
        input_output_aliases={} if before is None else {6: 0},
        scratch_shapes=[pltpu.VMEM((2, LANES, 7 * LANES), F32)],
        compiler_params=pltpu.CompilerParams(vmem_limit_bytes=48 * MIB),
        cost_estimate=SLIGHT,
        name="attend_back",
    )(qkv, qkv, qkv, do, powers, recips, *extra)


def gelu_pair(u):
    c = 0.7978845608028654
    sq = u * u
    th = jnp.tanh(u * (c + (c * 0.044715) * sq))
    half = 0.5 * th + 0.5
    slope = half + (0.5 * u) * (1.0 - th * th) * (c + (3.0 * c * 0.044715) * sq)
    return u * half, slope


def feed_kernel(core_ref, x_ref, o_ref, dyl_ref, gain_ref, wo_ref, wi_ref, wf_ref,
                f_ref, mid_ref, dmid_ref, do_ref, dml_ref, wi_keep, wi_send, wf_keep, wf_send, gg_ref,
                a2_ref, a2t_ref, du_ref):
    step = pl.program_id(0)
    rows = x_ref.shape[0]
    chunk = ROWS

    @pl.when(step == 0)
    def _():
        wo = square(wo_ref)
        for at in range(0, rows, chunk):
            here = pl.ds(at, chunk)
            mid = x_ref[here].astype(F32) + mm(o_ref[here], wo)
            mid_ref[here] = mid
            a2_ref[here] = (mid * inverse_rms(mid) * gain_ref[...]).astype(BF16)
            dmid_ref[here] = jnp.zeros((chunk, WIDTH), F32)
        a2t_ref[...] = a2_ref[...].T

    wi = square(wi_ref)
    wf = square(wf_ref)
    for at in range(0, rows, chunk):
        here = pl.ds(at, chunk)
        u = mm(a2_ref[here], wi)
        da = mm_nt(dyl_ref[here], wf)
        f, slope = gelu_pair(u)
        f = f.astype(BF16)
        du = (da * slope).astype(BF16)
        f_ref[here] = f
        du_ref[here] = du
        dmid_ref[here] += mm_nt(du, wi)
    split_store(core_ref, mm_tn(f_ref[...], dyl_ref[...]), wf_keep, wf_send)
    split_store(core_ref, mm(a2t_ref[...], du_ref[...]), wi_keep, wi_send)

    @pl.when(step == pl.num_programs(0) - 1)
    def _():
        gg = jnp.zeros((1, WIDTH), F32)
        wo = square(wo_ref)
        for at in range(0, rows, chunk):
            here = pl.ds(at, chunk)
            dm, dg = norm_back(mid_ref[here], gain_ref[...], dmid_ref[here])
            gg += dg
            dm = dm + dyl_ref[here].astype(F32)
            dmid_ref[here] = dm
            low = dm.astype(BF16)
            dml_ref[here] = low
            do_ref[here] = mm_nt(low, wo).astype(BF16)
        gg_ref[...] = gg


def feed(core, x, o, dyl, gain, rest):
    rows = x.shape[0]
    parts, _, per, _ = rest.shape
    group = WIDTH // (4 * per) if parts > 1 else 1
    wf_map = (lambda t: (t, 0, 0, 0)) if parts > 1 else (lambda t: (0, t, 0, 0))
    wf_block = (group, 4, per, WIDTH) if parts > 1 else (1, 1, per, WIDTH)
    half = per // 2
    wf_half = pl.BlockSpec(wf_block[:2] + (half, WIDTH), wf_map)
    wi_half = pl.BlockSpec((parts, 1, half, WIDTH), lambda t: (0, t, 0, 0))
    halves = jax.ShapeDtypeStruct((parts, 4, half, WIDTH), BF16)
    one = (parts, 1, per, WIDTH)
    whole = lambda shape: pl.BlockSpec(shape, lambda t: (0,) * len(shape), pipeline_mode=pl.Buffered(1))
    full = (rows, WIDTH)
    return pl.pallas_call(
        feed_kernel,
        grid=(FF // WIDTH,),
        in_specs=[
            pl.BlockSpec(memory_space=pltpu.SMEM),
            whole(full),
            whole(full),
            whole(full),
            whole((1, WIDTH)),
            pl.BlockSpec(one, lambda t: (0, 8, 0, 0), pipeline_mode=pl.Buffered(1)),
            pl.BlockSpec(one, lambda t: (0, 4 + t, 0, 0)),
            pl.BlockSpec(wf_block, wf_map),
        ],
        out_specs=[
            pl.BlockSpec(full, lambda t: (0, t)),
            whole(full),
            whole(full),
            whole(full),
            whole(full),
            wi_half,
            wi_half,
            wf_half,
            wf_half,
            whole((1, WIDTH)),
        ],
        out_shape=[
            jax.ShapeDtypeStruct((rows, FF), BF16),
            jax.ShapeDtypeStruct(full, F32),
            jax.ShapeDtypeStruct(full, F32),
            jax.ShapeDtypeStruct(full, BF16),
            jax.ShapeDtypeStruct(full, BF16),
            halves,
            halves,
            halves,
            halves,
            jax.ShapeDtypeStruct((1, WIDTH), F32),
        ],
        scratch_shapes=[
            pltpu.VMEM(full, BF16),
            pltpu.VMEM((WIDTH, rows), BF16),
            pltpu.VMEM(full, BF16),
        ],
        compiler_params=pltpu.CompilerParams(vmem_limit_bytes=48 * MIB),
        cost_estimate=SLIGHT,
        name="feed",
    )(core, x, o, dyl, gain, rest, rest, rest)


def block_out_kernel(mid_ref, f_ref, wf_ref, *refs):
    out_ref, acc_ref = refs[-2:]
    step = pl.program_id(0)

    @pl.when(step == 0)
    def _():
        acc_ref[...] = mid_ref[...]

    acc_ref[...] += mm(f_ref[...], square(wf_ref))

    @pl.when(step == pl.num_programs(0) - 1)
    def _():
        out_ref[...] = acc_ref[...].astype(BF16)


def block_out(mid, f, rest, after=()):
    rows = mid.shape[0]
    parts, _, per, _ = rest.shape
    full = (rows, WIDTH)
    whole = pl.BlockSpec(full, lambda t: (0, 0), pipeline_mode=pl.Buffered(1))
    if parts > 1:
        wf_spec = pl.BlockSpec((WIDTH // (4 * per), 4, per, WIDTH), lambda t: (t, 0, 0, 0))
    else:
        wf_spec = pl.BlockSpec((1, 1, per, WIDTH), lambda t: (0, t, 0, 0))
    return pl.pallas_call(
        block_out_kernel,
        grid=(FF // WIDTH,),
        in_specs=[whole, pl.BlockSpec(full, lambda t: (0, t)), wf_spec]
        + [pl.BlockSpec(memory_space=pl.ANY)] * len(after),
        out_specs=whole,
        out_shape=jax.ShapeDtypeStruct(full, BF16),
        scratch_shapes=[pltpu.VMEM(full, F32)],
        compiler_params=pltpu.CompilerParams(vmem_limit_bytes=48 * MIB),
        cost_estimate=SLIGHT,
        name="block_out",
    )(mid, f, rest, *after)


class Links:
    def __init__(self):
        dp, fsdp = lax.axis_index("dp"), lax.axis_index("fsdp")
        self.core, self.y = dp % 2, dp // 2
        self.x, self.z = fsdp % 2, fsdp // 2

    def swap(self, value, core=0, y=0, x=0, z=0):
        dp_bits, fsdp_bits = 2 * y + core, 2 * z + x
        pairs = [
            (8 * d + f, 8 * (d ^ dp_bits) + (f ^ fsdp_bits)) for d in range(4) for f in range(8)
        ]
        return lax.ppermute(value, ("dp", "fsdp"), pairs)


def place_kernel(at_ref, *refs):
    pieces, out_ref = refs[:-1], refs[-1]
    for n, piece in enumerate(pieces):
        for slot in range(4):
            spot = 3 * (4 * n + slot)
            out_ref[at_ref[spot], at_ref[spot + 1], at_ref[spot + 2]] = piece[slot]


def place(at, pieces, parts, kinds):
    half = pieces[0].shape[1]
    out = pl.pallas_call(
        place_kernel,
        in_specs=[pl.BlockSpec(memory_space=pltpu.SMEM)]
        + [pl.BlockSpec(memory_space=pltpu.VMEM)] * len(pieces),
        out_specs=pl.BlockSpec(memory_space=pltpu.VMEM),
        out_shape=jax.ShapeDtypeStruct((parts, kinds, 2, half, WIDTH), BF16),
        compiler_params=pltpu.CompilerParams(vmem_limit_bytes=24 * MIB),
        name="place",
    )(at, *pieces)
    return out.reshape(parts, kinds, 2 * half, WIDTH)


def fetch_weights(links, shard):
    half = shard.shape[1] // 2
    mine = lax.dynamic_slice_in_dim(shard, links.core * half, half, axis=1)
    both = mine[0]
    one = lax.dynamic_index_in_dim(mine, 1 + links.y, 0, keepdims=False)
    first = jnp.stack([both, one])
    level = jnp.stack([first, links.swap(first, z=2)], axis=1)
    more = links.swap(level, z=1)
    level_a = jnp.concatenate([level[1], more[1]])
    level_b = jnp.concatenate([level[0], more[0]])
    across_a = links.swap(level_a, x=1)
    over_a = links.swap(level_a, y=1)
    across_b = links.swap(level_b, x=1)
    over_across = links.swap(across_a, y=1)
    pieces, at = [], []
    for value, kind, x_bit in (
        (level_a, 1 + links.y, 0),
        (level_b, 0, 0),
        (across_a, 1 + links.y, 1),
        (over_a, 2 - links.y, 0),
        (across_b, 0, 1),
        (over_across, 2 - links.y, 1),
    ):
        for piece, core in ((value, links.core), (links.swap(value, core=1), 1 - links.core)):
            pieces.append(piece)
            for slot in range(4):
                z = links.z ^ ((slot % 2) * 2 + slot // 2)
                at += [2 * z + (links.x ^ x_bit), kind, core]
    at = jnp.stack([jnp.asarray(v, jnp.int32) for v in at])
    return place(at, pieces, 8, 3)


def pick(value, index, axis):
    return lax.dynamic_index_in_dim(value, index, axis, keepdims=False)


def added(a, b):
    return a.astype(F32) + b.astype(F32)


def by_x(value):
    return value.reshape((4, 2) + value.shape[1:])


def lanes(value, which):
    cut = WIDTH // 2
    return lax.dynamic_slice_in_dim(value, which * cut, cut, axis=value.ndim - 1)


class GradSum:
    def __init__(self, links, keep_a, send_a, keep_b, send_b):
        self.links = links
        self.a, self.b = keep_a, keep_b
        self.sent = (send_a, send_b)
        self.got = tuple(links.swap(v, core=1) for v in self.sent)

    def wait(self, *others):
        self.got = tuple(lax.optimization_barrier(self.got + others))[: len(self.got)]

    def first(self):
        links, a, b = self.links, self.a, self.b
        got_a, got_b = self.got
        go_a = added(lanes(a, 1 - links.y), lanes(got_a, 1 - links.y)).astype(BF16)
        go_b = added(pick(by_x(b), 1 - links.x, 1), pick(by_x(got_b), 1 - links.x, 1)).astype(BF16)
        self.sent = (go_a, go_b)
        self.got = (links.swap(go_a, y=1), links.swap(go_b, x=1))
        self.a = added(lanes(a, links.y), lanes(got_a, links.y)).astype(BF16)
        self.b = added(pick(by_x(b), links.x, 1), pick(by_x(got_b), links.x, 1)).astype(BF16)

    def second(self):
        links, a, b = self.links, self.a, self.b
        got_a, got_b = self.got
        go_a = added(pick(by_x(a), 1 - links.x, 1), pick(by_x(got_a), 1 - links.x, 1)).astype(BF16)
        go_b = added(lanes(b, 1 - links.y), lanes(got_b, 1 - links.y)).astype(BF16)
        self.sent = (go_a, go_b)
        self.got = (links.swap(go_a, x=1), links.swap(go_b, y=1))
        self.a = added(pick(by_x(a), links.x, 1), pick(by_x(got_a), links.x, 1)).astype(BF16)
        self.b = added(lanes(b, links.y), lanes(got_b, links.y)).astype(BF16)

    def third(self):
        links = self.links
        got_a, got_b = self.got

        def at_z(z):
            a = added(pick(self.a, z, 0), pick(got_a, z, 0))
            b = added(pick(self.b, z, 0), pick(got_b, z, 0))
            return jnp.concatenate([a, b])

        self.sent = tuple(at_z(links.z ^ bits).astype(BF16) for bits in (2, 3, 1))
        self.got = tuple(links.swap(v, z=bits) for v, bits in zip(self.sent, (2, 3, 1)))
        self.total = at_z(links.z)

    def third_by_collective(self):
        got_a, got_b = self.got
        total = jnp.concatenate([added(self.a, got_a), added(self.b, got_b)], axis=1).astype(BF16)
        kinds, half, cut = total.shape[1:]
        self.total = total
        groups = [[2 * z + x for z in range(4)] for x in range(2)]
        self.mine = lax.psum_scatter(
            total.reshape(-1, cut), "fsdp", scatter_dimension=0, tiled=True, axis_index_groups=groups
        )

    def gather(self, *others):
        mine = tie(self.mine, *others)
        return lax.all_gather(mine, "dp", axis=0, tiled=True).reshape((4,) + self.total.shape[1:])

    def sum_up(self):
        total = self.total
        for part in self.got:
            total = total + part.astype(F32)
        self.total = total.astype(BF16)

    def last(self, *others):
        links = self.links
        total = self.total
        other = tie(links.swap(total, y=1), *others)
        left = jnp.where(links.y == 0, total, other)
        right = jnp.where(links.y == 0, other, total)
        mine = jnp.concatenate([left, right], axis=-1)
        return mine, links.swap(mine, core=1)


def tie(value, *others):
    return lax.optimization_barrier((value,) + others)[0]


def sum_small(links, value, steps, marks=()):
    for n, step in enumerate(steps):
        if n < len(marks):
            value = tie(value, *marks[n])
        value = value + links.swap(value, **step)
    return value


FSDP_STEPS = (dict(z=2), dict(z=1), dict(x=1))
ALL_STEPS = (dict(core=1), dict(x=1), dict(y=1), dict(z=2), dict(z=1))


def moments(weight, first, second, grad):
    first_new = BETA_ONE * first + (1.0 - BETA_ONE) * grad
    second_new = BETA_TWO * second + (1.0 - BETA_TWO) * grad * grad
    root = jnp.sqrt(second_new * (1.0 / (1.0 - BETA_TWO**STEP)))
    direction = first_new * (1.0 / (1.0 - BETA_ONE**STEP)) / (root + ADAM_EPS) + DECAY * weight
    return (first_new, second_new, direction)


def update_piece(weight_ref, first_ref, second_ref, grads, m_out, v_out, r_out):
    half = grads[0].shape[0]
    squares = [jnp.zeros((1, WIDTH), F32)] * 2
    for part in range(2):
        here = pl.ds(part * half, half)
        weight = weight_ref[here]
        m_new, v_new, r = moments(weight, first_ref[here], second_ref[here], grads[part])
        m_out[here] = m_new
        v_out[here] = v_new
        r_out[here] = r
        squares[0] += jnp.sum(weight * weight, axis=0, keepdims=True)
        squares[1] += jnp.sum(r * r, axis=0, keepdims=True)
    return jnp.concatenate(squares, axis=0)


def update_attn_kernel(core_ref, other_ref, mine_ref, theirs_ref, p_ref, m_ref, v_ref,
                       m_out, v_out, last_out, r_out, sum_out):
    first = core_ref[0] == 0
    sums = other_ref[...]
    lane = lax.broadcasted_iota(jnp.int32, sums.shape, 1)
    for n in range(4):
        mine, theirs = mine_ref[n].astype(F32), theirs_ref[n].astype(F32)
        grads = (jnp.where(first, mine, theirs), jnp.where(first, theirs, mine))
        second_out = v_out.at[n] if n < 3 else last_out
        squares = update_piece(
            p_ref.at[n], m_ref.at[n], v_ref.at[n], grads, m_out.at[n], second_out, r_out.at[n]
        )
        sums = jnp.where(lane == n, jnp.sum(squares, axis=1, keepdims=True), sums)
    sum_out[...] = sums


def update_attn(core, other, mine, theirs, arrays):
    like = jax.ShapeDtypeStruct(arrays[0].shape, F32)
    per = like.shape[1]
    whole = lambda shape: pl.BlockSpec(shape, lambda k: (0,) * len(shape))
    shapes = [like.shape, (3, per, WIDTH), (per, WIDTH), like.shape, other.shape]
    return pl.pallas_call(
        update_attn_kernel,
        grid=(1,),
        in_specs=[pl.BlockSpec(memory_space=pltpu.SMEM), whole(other.shape)]
        + [whole(mine.shape)] * 2
        + [whole(like.shape)] * 3,
        out_specs=[whole(shape) for shape in shapes],
        out_shape=[jax.ShapeDtypeStruct(shape, F32) for shape in shapes],
        compiler_params=pltpu.CompilerParams(vmem_limit_bytes=60 * MIB),
        cost_estimate=SLIGHT,
        name="update_attn",
    )(core, other, mine, theirs, *arrays)


def update_feed_kernel(out_grad, in_grad, *refs):
    arrays, (sum_out,) = refs[:12], refs[12:]
    for n, grad in enumerate((out_grad, in_grad)):
        pieces = [grad[place, 0].astype(F32) for place in range(4)]
        grads = [jnp.concatenate([pieces[part], pieces[2 + part]], axis=1) for part in range(2)]
        ins, outs = arrays[3 * n : 3 * n + 3], arrays[6 + 3 * n : 9 + 3 * n]
        sum_out[0, n] = update_piece(*ins, grads, *outs)


def update_feed(grads, out_arrays, in_arrays):
    per = in_arrays[0].shape[0]
    quarter = (4, 1) + grads.shape[2:]
    out_block = pl.BlockSpec((per, WIDTH), lambda k: (k, 0))
    in_block = pl.BlockSpec((per, WIDTH), lambda k: (0, k))
    blocks = [out_block] * 3 + [in_block] * 3
    return pl.pallas_call(
        update_feed_kernel,
        grid=(4,),
        in_specs=[
            pl.BlockSpec(quarter, lambda k: (0, k, 0, 0)),
            pl.BlockSpec(quarter, lambda k: (0, k + 4, 0, 0)),
        ]
        + blocks,
        out_specs=blocks + [pl.BlockSpec((1, 2, 2, WIDTH), lambda k: (k, 0, 0, 0))],
        out_shape=[jax.ShapeDtypeStruct(v.shape, F32) for v in out_arrays + in_arrays]
        + [jax.ShapeDtypeStruct((4, 2, 2, WIDTH), F32)],
        compiler_params=pltpu.CompilerParams(vmem_limit_bytes=60 * MIB),
        cost_estimate=SLIGHT,
        name="update_feed",
    )(grads, grads, *out_arrays, *in_arrays)


def apply_kernel(sums_ref, gains_p, gains_r, table_p, table_r, attn_w, attn_r, in_w, in_r, out_w, out_r,
                 attn_ref, in_ref, out_ref, gains_ref, table_ref, norms_ref):
    step = pl.program_id(0)
    norms = jnp.sqrt(sums_ref[...])
    scale = RATE * (norms[0:1] / (norms[1:2] + ADAM_EPS))
    lane = lax.broadcasted_iota(jnp.int32, scale.shape, 1)
    take = lambda n: jnp.sum(jnp.where(lane == n, scale, 0.0), axis=1, keepdims=True)
    attn_ref[0] = attn_w[0] - take(step) * attn_r[0]
    in_ref[...] = in_w[...] - take(4) * in_r[...]
    out_ref[...] = out_w[...] - take(5) * out_r[...]

    @pl.when(step == 0)
    def _():
        for n in range(2):
            gains_ref[n : n + 1] = gains_p[n : n + 1] - take(6 + n) * gains_r[n : n + 1]
        table_ref[...] = table_p[...] - take(8) * table_r[...]
        square_of = (norms_ref.shape[0], scale.shape[1])
        here = lax.broadcasted_iota(jnp.int32, square_of, 0) == lax.broadcasted_iota(jnp.int32, square_of, 1)
        for n in range(2):
            column = jnp.where(here, jnp.broadcast_to(norms[n : n + 1], square_of), 0.0)
            norms_ref[:, n : n + 1] = jnp.sum(column, axis=1, keepdims=True)


def apply(sums, gains, table, attn, ffin, ffout):
    per = ffin[0].shape[0]
    whole = lambda v: pl.BlockSpec(v.shape, lambda k: (0,) * len(v.shape))
    specs = [
        pl.BlockSpec((1, per, WIDTH), lambda k: (k, 0, 0)),
        pl.BlockSpec((per, WIDTH), lambda k: (0, k)),
        pl.BlockSpec((per, WIDTH), lambda k: (k, 0)),
    ]
    norms = jax.ShapeDtypeStruct((9, 2), F32)
    return pl.pallas_call(
        apply_kernel,
        grid=(4,),
        in_specs=[whole(v) for v in (sums, *gains, *table)] + [spec for spec in specs for _ in range(2)],
        out_specs=specs + [whole(gains[0]), whole(table[0]), whole(norms)],
        out_shape=[jax.ShapeDtypeStruct(v[0].shape, F32) for v in (attn, ffin, ffout, gains, table)] + [norms],
        compiler_params=pltpu.CompilerParams(vmem_limit_bytes=60 * MIB),
        cost_estimate=SLIGHT,
        name="apply",
    )(sums, *gains, *table, *attn, *ffin, *ffout)


def row_labels(lengths):
    ends = jnp.cumsum(lengths, axis=1)
    places = jnp.arange(ROWS, dtype=jnp.int32)
    labels = jnp.sum((places[None, :, None] >= ends[:, None, :]).astype(jnp.int32), axis=2)
    return labels, places[None, :] < ends[:, -1:]


def label_masks(labels, count):
    codes = jnp.arange(HD)
    equal = labels[:, :, None] == codes
    keys = jnp.where(equal | (codes >= count), 0.0, 1.0).astype(BF16)
    queries = jnp.where(equal, -FAR, 0.0).astype(BF16)
    none = jnp.zeros_like(keys)
    sides = lambda v: jnp.stack(
        [jnp.concatenate([none, v], axis=-1), jnp.concatenate([v, none], axis=-1)], axis=1
    )
    return sides(keys), sides(queries)


def body(
    tokens, cotangent, seg_lengths, bucket_of,
    attn_w, attn_m, attn_v, ffin_w, ffin_m, ffin_v, ffout_w, ffout_m, ffout_v,
    gains, gains_m, gains_v, table, table_m, table_v,
):
    fsdp = lax.axis_size("fsdp")
    dp = lax.axis_size("dp")
    both = ("fsdp", "dp")
    batches, count, width = tokens.shape
    rows = batches * count
    blocks = rows // ROWS
    per = attn_w.shape[1]
    direct = per % 32 == 0
    paired = direct and fsdp == 8 and dp == 4
    links = Links() if paired else None
    core = (links.core if paired else jnp.int32(0)).reshape(1)

    me = lax.axis_index("dp")

    def spread(shard):
        flat = shard.reshape(-1, WIDTH)
        size = flat.shape[0] // dp
        mine = lax.dynamic_slice_in_dim(flat, me * size, size, axis=0)
        return lax.all_gather(mine, both, axis=0, tiled=True).reshape((fsdp,) + shard.shape)

    def whole_of(gathered):
        kinds = gathered.shape[1]
        return gathered.transpose(1, 0, 2, 3).reshape(1, kinds, WIDTH, WIDTH)

    attn_low = attn_w.astype(BF16)
    ffin_low = ffin_w.astype(BF16).reshape(per, 4, WIDTH).transpose(1, 0, 2)
    ffout_low = ffout_w.astype(BF16).reshape(4, per, WIDTH)
    qkv_w = fetch_weights(links, attn_low[:3]) if paired else spread(attn_low[:3])
    rest_w = spread(jnp.concatenate([ffout_low, ffin_low, attn_low[3:]], axis=0))
    if not direct:
        qkv_w = whole_of(qkv_w)
        wf_all = rest_w[:, :4].reshape(1, 4, WIDTH, WIDTH)
        rest_w = jnp.concatenate([wf_all, whole_of(rest_w[:, 4:])], axis=1)
    small = jnp.concatenate([gains.reshape(-1), table.reshape(-1)]).astype(BF16)
    if paired:
        own = jnp.arange(fsdp)[:, None] == lax.axis_index("fsdp")
        small = sum_small(links, jnp.where(own, small[None].astype(F32), 0.0), FSDP_STEPS).astype(BF16)
    else:
        small = lax.all_gather(small, "fsdp", axis=0)
    gain_full = small[:, : 2 * per].reshape(fsdp, 2, per).transpose(1, 0, 2).reshape(2, 1, width).astype(F32)
    table_full = small[:, 2 * per :].reshape(BUCKETS, HEADS)

    padded = jnp.concatenate([bucket_of, jnp.full((1,), -1, jnp.int32)])
    padded = jnp.roll(padded[::-1], -(OFFS - 1 - 7 * LANES + 1))
    onehot = (padded[None, :] == jnp.arange(BUCKETS, dtype=jnp.int32)[:, None]).astype(BF16)
    off_rows = lax.dot_general(
        table_full, onehot, (((0,), (0,)), ((), ())), preferred_element_type=F32
    ).reshape(PAIRS, 2, OFFS)

    labels, valid = row_labels(seg_lengths.reshape(blocks, -1))
    mask_keys, mask_queries = label_masks(labels, seg_lengths.shape[-1] + 1)
    x = tokens.reshape(rows, width)
    dyl = jnp.where(valid.reshape(rows, 1), cotangent.reshape(rows, width), jnp.zeros((), BF16))

    qkv, a1 = project(x, gain_full[0], qkv_w)
    qkv = qkv.reshape(3, blocks, ROWS, width)
    o, powers, recips = attend(off_rows, mask_keys, mask_queries, qkv)
    f, mid, dmid, do, dml, wi_keep, wi_send, wf_keep, wf_send, gg2 = feed(
        core, x, o.reshape(rows, width), dyl, gain_full[1], rest_w
    )
    do = do.reshape(blocks, ROWS, width)

    def small_grads(gg1, gt):
        grad_table = lax.dot_general(
            onehot.astype(F32), gt.reshape(HEADS, OFFS), (((1,), (1,)), ((), ())),
            preferred_element_type=F32, precision=lax.Precision.HIGHEST,
        )
        grad_gains = jnp.concatenate([gg1, gg2], axis=0).reshape(2, fsdp, per).transpose(1, 0, 2).reshape(fsdp, -1)
        return jnp.concatenate([grad_gains, grad_table.reshape(fsdp, -1)], axis=1)

    o = o.reshape(rows, width)
    parts = qkv_w.shape[0]
    if paired:
        feed_sum = GradSum(links, wf_keep, wf_send, wi_keep, wi_send)
        dqkv, gt0 = attend_back(qkv, do, powers, recips, 0, 2)
        feed_sum.wait(gt0)
        feed_sum.first()
        dqkv, gt1 = attend_back(qkv, do, powers, recips, 2, 2, dqkv, feed_sum.sent)
        dqkv, gt2 = attend_back(qkv, do, powers, recips, 4, 2, dqkv)
        dqkv = dqkv.reshape(3, rows, width)
        out = block_out(mid, f, rest_w, (gt2,))
        feed_sum.wait(out)
        feed_sum.second()
        attn_sets = list(weight_grads(core, dqkv, dml, a1, o, parts, feed_sum.sent))
        feed_sum.wait(attn_sets[0])
        feed_sum.third_by_collective()
        attn_sets[1], attn_sets[3] = (tie(attn_sets[n], feed_sum.total) for n in (1, 3))
        attn_sum = GradSum(links, *attn_sets)
        attn_sum.first()
        gin, gg1 = input_grad(dqkv, x, gain_full[0], dmid, qkv_w, attn_sum.sent)
        attn_sum.wait(gg1)
        attn_sum.second()
        gt = jnp.concatenate([gt0, gt1, gt2])
        grad_small = sum_small(links, small_grads(gg1, gt), ALL_STEPS[:1], [attn_sum.sent])
        attn_sum.wait(grad_small)
        marks = []
        attn_sum.third()
        marks += [attn_sum.sent] * 2
        feed_grads = feed_sum.gather(*attn_sum.sent)
        attn_sum.sum_up()
        feed_grads = tie(feed_grads, attn_sum.total)
    else:
        dqkv, gt = attend_back(qkv, do, powers, recips, 0, PAIRS)
        dqkv = dqkv.reshape(3, rows, width)
        out = block_out(mid, f, rest_w)
        attn_sets = weight_grads(core, dqkv, dml, a1, o, parts)
        gin, gg1 = input_grad(dqkv, x, gain_full[0], dmid, qkv_w)
    def parts_of(grad):
        kinds = grad.shape[1]
        return grad.reshape(kinds, fsdp, per, WIDTH).transpose(1, 0, 2, 3)

    def gather_sum(grad):
        kinds = grad.shape[1]
        flat = grad.reshape(fsdp * kinds * per, WIDTH)
        mine = lax.psum_scatter(flat, both, scatter_dimension=0, tiled=True)
        return lax.all_gather(mine, "dp", axis=0, tiled=True).reshape(kinds, per, WIDTH).astype(F32)

    if not paired:
        dwf = jnp.concatenate([wf_keep, wf_send], axis=2).reshape(fsdp, 4, per, WIDTH)
        dwi = jnp.concatenate([wi_keep, wi_send], axis=2)
        dw = [jnp.concatenate(attn_sets[n : n + 2], axis=2) for n in (0, 2)]
        dw = jnp.concatenate(dw, axis=1)
        if not direct:
            dwi, dw = parts_of(dwi), parts_of(dw)
        half, cut = per // 2, WIDTH // 2
        feed_grads = gather_sum(jnp.concatenate([dwf, dwi], axis=1)).reshape(8, 2, half, 2, cut)
        feed_grads = feed_grads.transpose(3, 1, 0, 2, 4).reshape(4, 8, half, cut)
        attn_grads = gather_sum(dw)
        attn_mine, attn_theirs = attn_grads[:, :half], attn_grads[:, half:]
        marks = []

    if not paired:
        grad_small = small_grads(gg1, gt)

    out_m, out_v, out_r, in_m, in_v, in_r, feed_sq = update_feed(
        feed_grads, (ffout_w, ffout_m, ffout_v), (ffin_w, ffin_m, ffin_v)
    )
    if paired:
        attn_mine, attn_theirs = attn_sum.last(feed_sq)
    feed_sq = jnp.sum(feed_sq, axis=(0, 3))[::-1].T
    if paired:
        grad_small = sum_small(links, grad_small, ALL_STEPS[1:], marks)
    else:
        grad_small = lax.psum(grad_small, ("dp", "fsdp"))
    grad_small = lax.dynamic_index_in_dim(grad_small, lax.axis_index("fsdp"), 0, keepdims=False)

    flat = lambda a, b: jnp.concatenate([a.reshape(-1), b.reshape(-1)])
    small_p = flat(gains, table)
    small_m, small_v, small_r = moments(small_p, flat(gains_m, table_m), flat(gains_v, table_v), grad_small)
    kind = jnp.minimum(jnp.arange(small_p.shape[0]) // per, 2)
    member = kind[None, :] == jnp.arange(3)[:, None]
    squares = lambda v: jnp.sum(jnp.where(member, (v * v)[None], 0.0), axis=1)

    def unpack(v):
        return v[: 2 * per].reshape(2, per), v[2 * per :].reshape(table.shape)

    gains_r, table_r = unpack(small_r)
    gains_m_new, table_m_new = unpack(small_m)
    gains_v_new, table_v_new = unpack(small_v)

    other = jnp.concatenate([feed_sq, jnp.stack([squares(small_p), squares(small_r)])], axis=1)
    other = jnp.pad(other, ((0, 0), (4, LANES - 9)))
    attn_new_m, attn_new_v, out_new_v, attn_r, sums = update_attn(
        core, other, attn_mine, attn_theirs, (attn_w, attn_m, attn_v)
    )
    sums = sum_small(links, sums, FSDP_STEPS) if paired else lax.psum(sums, "fsdp")
    attn_new, ffin_new, ffout_new, gains_new, table_new, norms = apply(
        sums, (gains, gains_r), (table, table_r), (attn_w, attn_r), (ffin_w, in_r), (ffout_w, out_r)
    )
    return (
        out.reshape(tokens.shape),
        gin.reshape(tokens.shape),
        attn_new, attn_new_m, attn_new_v, out_new_v,
        ffin_new, in_m, in_v,
        ffout_new, out_m, out_v,
        gains_new, gains_m_new, gains_v_new,
        table_new, table_m_new, table_v_new,
        norms,
    )


def solution(mesh):
    batch = P(None, ("dp", "fsdp"), None)
    mid_dim = P(None, "fsdp", None)
    first = P("fsdp", None)
    last = P(None, "fsdp")
    in_specs = (batch, batch, batch, P()) + (mid_dim,) * 3 + (first,) * 6 + (last,) * 3 + (first,) * 3
    out_specs = (batch, batch) + (mid_dim,) * 3 + (first,) * 7 + (last,) * 3 + (first,) * 3 + (P(),)
    return jax.shard_map(body, mesh=mesh, in_specs=in_specs, out_specs=out_specs, check_vma=False)
```
